512 devices in a mesh: res: 64 (over y, z_lo, x), seq: 8 (over z_hi, core).
Axes of the slice: x: 4, y: 8, z: 8 (z_hi: 4, z_lo: 2; z = z_hi * 2 + z_lo), core: 2. Of those that a mesh axis runs over, the one named last changes fastest.
Arguments:
- aligned_chain_embedding: bfloat16 [512, 768, 256], P('seq', 'res'), may hold values from -6 to 6
- presence_indicator: int32 [512, 768], P('seq', 'res'), may hold values from 0 to 1, as said below
- outer_lhs_embedding: bfloat16 [256, 32], replicated, may hold values from -0.375 to 0.375
- outer_rhs_embedding: bfloat16 [256, 32], replicated, may hold values from -0.375 to 0.375
- final_projection_matrix: bfloat16 [1024, 128], replicated, may hold values from -1 to 1
- final_offset: float32 [128], replicated, may hold values from -3 to 3
Outputs:
- pair: float32 [768, 768, 128], P('res', 'seq')
The draws below stay inside these ranges and needn't reach their ends.
Inputs may be any that keep to these rules, and one draw needn't show every extreme that they name: `presence_indicator`: 0 or 1 for each sequence and residue.
All inputs are finite; a program needn't handle non-finite values.
Results may differ from the reference program's by a relative error of at most 0.0075.
Values may be sent and summed in bfloat16 or wider, within the bound.
No kernel may reach another device: no remote copies, remote signals or barrier semaphores. Data moves between devices by JAX's collectives and lax.ppermute only.
A program may use at most 64 MiB of HBM per device.

```python
import jax
import jax.numpy as jnp
from jax import lax

EMBED_DEPTH = 256
PROJ_WIDTH = 32
PAIR = 128
SEQ_DEV = 64
RES_DEV = 12
ALIGNED_CHAINS = 512
CHAIN_LENGTH = 768
N_SEQ = 8


def draw_presence_indicator(key, part):
    key = jax.random.fold_in(key, 7)
    ticket = jax.random.randint(key, (ALIGNED_CHAINS, CHAIN_LENGTH), 0, 1000)
    order = jnp.arange(ALIGNED_CHAINS, dtype=jnp.int32)[:, None]
    limit = 900 - 600 * order // ALIGNED_CHAINS
    return (ticket < limit).astype(jnp.int32)


def draw_aligned_chain_embedding(key, part):
    key = jax.random.fold_in(key, 11)
    entry_key, level_key, pick_key = jax.random.split(key, 3)
    full_shape = (ALIGNED_CHAINS, CHAIN_LENGTH, EMBED_DEPTH)
    row_shape = (ALIGNED_CHAINS, CHAIN_LENGTH, 1)
    entries = jnp.clip(jax.random.normal(entry_key, full_shape, jnp.float32), -6.0, 6.0)
    levels = jnp.clip(jax.random.normal(level_key, row_shape, jnp.float32), -6.0, 6.0)
    flat_rows = jax.random.randint(pick_key, row_shape, 0, 6) == 0
    return jnp.where(flat_rows, jnp.broadcast_to(levels, full_shape), entries).astype(jnp.bfloat16)


def bell_draw(own_key, extent, scale, most, kind=jnp.bfloat16):
    return jnp.clip(scale * jax.random.normal(own_key, extent, jnp.float32), -most, most).astype(kind)


def setup_inputs(seed: int = 0) -> dict:
    keys = jax.random.split(jax.random.key(seed), 7)
    aligned_chain_embedding = draw_aligned_chain_embedding(jax.random.fold_in(keys[6], 71), 0)
    presence_indicator = draw_presence_indicator(jax.random.fold_in(keys[6], 71), 0)
    outer_lhs_embedding = bell_draw(keys[2], (EMBED_DEPTH, PROJ_WIDTH), EMBED_DEPTH ** -0.5, 0.375)
    outer_rhs_embedding = bell_draw(keys[3], (EMBED_DEPTH, PROJ_WIDTH), EMBED_DEPTH ** -0.5, 0.375)
    final_projection_matrix = bell_draw(keys[4], (PROJ_WIDTH * PROJ_WIDTH, PAIR), PROJ_WIDTH ** -0.5, 1.0)
    final_offset = bell_draw(keys[5], (PAIR,), 0.5, 3.0, jnp.float32)
    return {"aligned_chain_embedding": aligned_chain_embedding, "presence_indicator": presence_indicator, "outer_lhs_embedding": outer_lhs_embedding, "outer_rhs_embedding": outer_rhs_embedding, "final_projection_matrix": final_projection_matrix, "final_offset": final_offset}


def standardized_activations(aligned_chain_embedding):
    collected_entries = aligned_chain_embedding.astype(jnp.float32)
    center = lax.optimization_barrier(jnp.mean(collected_entries, axis=-1, keepdims=True))
    spread = lax.optimization_barrier(jnp.mean((collected_entries - center) ** 2, axis=-1, keepdims=True))
    return (collected_entries - center) * lax.rsqrt(spread + 1e-05)

def reference(aligned_chain_embedding, presence_indicator, outer_lhs_embedding, outer_rhs_embedding, final_projection_matrix, final_offset):
    standardized_source = standardized_activations(aligned_chain_embedding)
    weight_list = presence_indicator.astype(jnp.float32)
    left = (jnp.einsum('sik,kc->sic', standardized_source, outer_lhs_embedding.astype(jnp.float32), precision=lax.Precision.HIGHEST) * weight_list[:, :, None]).astype(jnp.bfloat16)
    right = (jnp.einsum('sik,kc->sic', standardized_source, outer_rhs_embedding.astype(jnp.float32), precision=lax.Precision.HIGHEST) * weight_list[:, :, None]).astype(jnp.bfloat16)
    mask_halfwidth = presence_indicator.astype(jnp.bfloat16)
    blocks = CHAIN_LENGTH // RES_DEV
    left_blocks = left.reshape(ALIGNED_CHAINS, blocks, RES_DEV, PROJ_WIDTH).transpose(1, 0, 2, 3)
    mask_blocks = mask_halfwidth.reshape(ALIGNED_CHAINS, blocks, RES_DEV).transpose(1, 0, 2)

    def one_block(items):
        left_rows, mask_row_slices = items
        total = jnp.zeros((RES_DEV, CHAIN_LENGTH, PAIR), jnp.float32)
        count = jnp.zeros((RES_DEV, CHAIN_LENGTH), jnp.float32)
        for group in range(N_SEQ):
            lo = group * SEQ_DEV
            left_part = left_rows[lo:lo + SEQ_DEV].astype(jnp.float32)
            right_part = right[lo:lo + SEQ_DEV].astype(jnp.float32)
            outer = jnp.einsum('sic,sje->ijce', left_part, right_part).astype(jnp.bfloat16)
            proj = jnp.dot(outer.reshape(RES_DEV * CHAIN_LENGTH, PROJ_WIDTH * PROJ_WIDTH), final_projection_matrix, preferred_element_type=jnp.float32).astype(jnp.bfloat16)
            total = total + proj.reshape(RES_DEV, CHAIN_LENGTH, PAIR).astype(jnp.float32)
            part_count = jnp.dot(mask_row_slices[lo:lo + SEQ_DEV].T, mask_halfwidth[lo:lo + SEQ_DEV], preferred_element_type=jnp.float32).astype(jnp.bfloat16)
            count = count + part_count.astype(jnp.float32)
        return total / (count[:, :, None] + 1.0) + final_offset
    pair = lax.map(one_block, (left_blocks, mask_blocks))
    return pair.reshape(CHAIN_LENGTH, CHAIN_LENGTH, PAIR)
```

```python
import numpy as np

import jax
import jax.numpy as jnp
from jax import lax
from jax.experimental import pallas as pl
from jax.experimental.pallas import tpu as pltpu
from jax.sharding import Mesh
from jax.sharding import PartitionSpec as P

F32, BF16 = jnp.float32, jnp.bfloat16
SIZES = (8, 2, 4, 4, 2)
AXES = ("y", "zl", "x", "zh", "core")
S, I, C, WIDTH, PAIR = 64, 12, 256, 32, 128
ROWS = 208
NT = (((1,), (1,)), ((), ()))
VMEM = pl.BlockSpec(memory_space=pltpu.VMEM)
SMEM = pl.BlockSpec(memory_space=pltpu.SMEM)


def one_hot(shape, match):
    row = lax.broadcasted_iota(jnp.int32, shape, 0)
    col = lax.broadcasted_iota(jnp.int32, shape, 1)
    return match(row, col).astype(F32).astype(BF16)


def dot(a, b, dims=(((1,), (0,)), ((), ()))):
    return lax.dot_general(a, b, dims, preferred_element_type=F32)


def project_kernel(x_ref, m_ref, wl_ref, wr_ref, l_ref, r_ref, rows, spread):
    x = x_ref[...].astype(F32)
    centred = x - jnp.sum(x, axis=-1, keepdims=True) * (1.0 / C)
    variance = jnp.sum(centred * centred, axis=-1, keepdims=True) * (1.0 / C)
    normed = centred * lax.rsqrt(variance + 1e-05)
    for s in range(S):
        for h in range(2):
            rows[h, s * 16 : s * 16 + I, :] = normed[s, :, h * 128 : h * 128 + 128]

    mask = m_ref[...].astype(F32)
    mask_twice = jnp.concatenate([mask, mask], axis=0).astype(BF16)
    mask_rows = dot(one_hot((16, I), lambda r, t: r == t), mask_twice, NT)
    mask_pairs = dot(one_hot((32, I), lambda r, t: r // 2 == t), mask_twice, NT)
    wl = dot(wl_ref[...], one_hot((WIDTH, 128), lambda r, t: r == t % WIDTH)).astype(BF16)
    wr = dot(
        one_hot((WIDTH, WIDTH), lambda r, t: t == 2 * (r % 16) + r // 16), wr_ref[...], NT
    ).astype(BF16)
    lane = lax.broadcasted_iota(jnp.int32, (8, 128), 1)
    block = lax.broadcasted_iota(jnp.int32, (S, 128), 1) // WIDTH
    low = lane < 64
    for g in range(I // 4):
        tile = None
        for k in range(4):
            i = 4 * g + k
            xi = jnp.concatenate([rows[h, pl.ds(i, S, stride=16), :] for h in range(2)], axis=1)
            high = xi.astype(BF16)
            rest = (xi - high.astype(F32)).astype(BF16)
            left = (dot(high, wl) + dot(rest, wl)) * mask[:, i : i + 1]
            tile = left if k == 0 else jnp.where(block == k, left, tile)
            high2 = jnp.concatenate([high, high], axis=0)
            rest2 = jnp.concatenate([rest, rest], axis=0)
            right = (dot(wr, high2, NT) + dot(wr, rest2, NT)) * mask_rows[i : i + 1, :]
            for e in range(2):
                part = jnp.where(low, right[e * 16 : e * 16 + 8], right[e * 16 + 8 : e * 16 + 16])
                spread[pl.ds(2 * i + e, 8, stride=24), :] = part
        l_ref[g * S : (g + 1) * S, :] = tile.astype(BF16)
    l_ref[192:208, :] = mask_rows.astype(BF16)
    r_ref[0:192, :] = spread[...].astype(BF16)
    low16 = lax.broadcasted_iota(jnp.int32, (16, 128), 1) < 64
    r_ref[192:208, :] = jnp.where(low16, mask_pairs[0:16], mask_pairs[16:32]).astype(BF16)


def pair_kernel(core_ref, lm_ref, lo_ref, rm_ref, ro_ref, w_ref, out_ref, rt, rmask, lmask, z):
    core = core_ref[0]
    low = lax.broadcasted_iota(jnp.int32, (ROWS, 128), 1) < 64
    low16 = lax.broadcasted_iota(jnp.int32, (16, 128), 1) < 64
    for zl, ref in enumerate((rm_ref, ro_ref)):
        for t in range(4):
            a = ref[2 * t + core].astype(F32)
            b = ref[2 * t + 1 - core].astype(F32)
            first = jnp.where(low, a, pltpu.roll(b, 64, 1)).astype(BF16)
            second = jnp.where(low, pltpu.roll(a, 64, 1), b).astype(BF16)
            cols = slice(t * 128, t * 128 + 128)
            rt[zl, 0:192, cols] = first[0:192]
            rt[zl, 192:384, cols] = second[0:192]
            rmask[zl, 0:16, cols] = first[192:208]
            rmask[zl, 16:32, cols] = second[192:208]
    for x0 in range(4):
        for t in range(4):
            a = lm_ref[x0, t, 192:208, :].astype(F32)
            b = lo_ref[x0, t, 192:208, :].astype(F32)
            lmask[x0 * 16 : x0 * 16 + 16, t * 128 : t * 128 + 128] = jnp.where(low16, a, b).astype(BF16)
    scale = [1.0 / (dot(rmask[zl], lmask[...], NT) + 1.0) for zl in range(2)]

    lanes = lax.broadcasted_iota(jnp.int32, (24, 128), 1)
    half = lanes < 64
    even = (lanes // WIDTH) % 2 == 0
    for x0 in range(4):
        rhs = jnp.concatenate(
            [
                jnp.concatenate([ref[x0, t, g * S : g * S + S, :] for g in range(3)], axis=1)
                for t in range(4)
                for ref in (lm_ref, lo_ref)
            ],
            axis=0,
        )
        for zl in range(2):
            outer = dot(rt[zl], rhs)
            left_rows = []
            for g in range(3):
                quads = [[], [], [], []]
                for q in range(4):
                    a = [
                        outer[(4 * q + n) * 24 : (4 * q + n) * 24 + 24, g * 128 : g * 128 + 128]
                        for n in range(4)
                    ]
                    a0 = jnp.where(half, a[0], pltpu.roll(a[2], 64, 1))
                    a1 = jnp.where(half, a[1], pltpu.roll(a[3], 64, 1))
                    a2 = jnp.where(half, pltpu.roll(a[0], 64, 1), a[2])
                    a3 = jnp.where(half, pltpu.roll(a[1], 64, 1), a[3])
                    quads[0].append(jnp.where(even, a0, pltpu.roll(a1, 32, 1)))
                    quads[1].append(jnp.where(even, pltpu.roll(a0, 96, 1), a1))
                    quads[2].append(jnp.where(even, a2, pltpu.roll(a3, 32, 1)))
                    quads[3].append(jnp.where(even, pltpu.roll(a2, 96, 1), a3))
                left_rows += [jnp.concatenate(quad, axis=1) for quad in quads]
            operand = jnp.concatenate(left_rows, axis=0).astype(BF16)
            wide = dot(operand, w_ref[...])
            for i in range(I):
                column = scale[zl][0:24, x0 * 16 + i : x0 * 16 + i + 1]
                for e in range(2):
                    z[e, i * 24 : i * 24 + 24, :] = (
                        wide[i * 24 : i * 24 + 24, e * 128 : e * 128 + 128] * column
                    )
            result = z[0, pl.ds(0, 144, stride=2), :] + z[1, pl.ds(1, 144, stride=2), :]
            out_ref[x0, zl] = result.astype(BF16)


def finish_kernel(zl_ref, pair_ref, offset_ref, out_ref):
    mine = zl_ref[0]
    offset = offset_ref[...]
    for zl in range(2):
        for x1 in range(4):
            block = pair_ref[x1, zl ^ mine].astype(F32) + offset
            for i in range(I):
                at = (zl * 4 + x1) * I
                out_ref[i, at : at + I, :] = block[i * I : i * I + I, :]


def swap(match):
    index = np.arange(int(np.prod(SIZES))).reshape(SIZES)
    return [(int(index[at]), int(index[match(*at)])) for at in np.ndindex(*SIZES)]


TRANSPOSE = swap(lambda y, zl, x, zh, c: (2 * zh + c, zl, x, y // 2, y % 2))
OTHER_ZL = swap(lambda y, zl, x, zh, c: (y, 1 - zl, x, zh, c))
OTHER_CORE = swap(lambda y, zl, x, zh, c: (y, zl, x, zh, 1 - c))


def spread_along(value, axis, count):
    return lax.all_to_all(
        jnp.broadcast_to(value[None], (count,) + value.shape), axis, 0, 0, tiled=True
    )


def after(value, earlier):
    return lax.optimization_barrier((value, earlier))[0]


def local(x, m, wl, wr, w, offset):
    left, right = pl.pallas_call(
        project_kernel,
        out_shape=[jax.ShapeDtypeStruct((ROWS, 128), BF16)] * 2,
        in_specs=[VMEM] * 4,
        out_specs=[VMEM] * 2,
        scratch_shapes=[pltpu.VMEM((2, S * 16, 128), F32), pltpu.VMEM((192, 128), F32)],
        compiler_params=pltpu.CompilerParams(vmem_limit_bytes=48 << 20),
    )(x, m, wl, wr)
    w2 = w.reshape(WIDTH, 16, 2, PAIR).transpose(1, 0, 2, 3).reshape(512, 2 * PAIR)

    right = lax.ppermute(right, AXES, TRANSPOSE)
    left = spread_along(left, "zh", 4)
    right = spread_along(after(right, left), "y", 8)
    right_other = lax.ppermute(right, AXES, OTHER_ZL)
    left = spread_along(after(left, right), "x", 4)
    left_other = lax.ppermute(left, AXES, OTHER_CORE)

    core = lax.axis_index("core").astype(jnp.int32).reshape(1)
    zl = lax.axis_index("zl").astype(jnp.int32).reshape(1)
    pairs = pl.pallas_call(
        pair_kernel,
        out_shape=jax.ShapeDtypeStruct((4, 2, 144, 128), BF16),
        in_specs=[SMEM] + [VMEM] * 5,
        out_specs=VMEM,
        scratch_shapes=[
            pltpu.VMEM((2, 384, 512), BF16),
            pltpu.VMEM((2, 32, 512), BF16),
            pltpu.VMEM((64, 512), BF16),
            pltpu.VMEM((2, 288, 128), F32),
        ],
        compiler_params=pltpu.CompilerParams(vmem_limit_bytes=48 << 20),
    )(core, left, left_other, right, right_other, w2)
    pairs = lax.all_to_all(pairs, "x", 0, 0, tiled=True)
    return pl.pallas_call(
        finish_kernel,
        out_shape=jax.ShapeDtypeStruct((I, 96, PAIR), F32),
        in_specs=[SMEM, VMEM, VMEM],
        out_specs=VMEM,
        compiler_params=pltpu.CompilerParams(vmem_limit_bytes=48 << 20),
    )(zl, pairs, offset.reshape(1, PAIR))


def solution(mesh):
    fine = Mesh(mesh.devices.reshape(SIZES), AXES)
    res, seq = ("y", "zl", "x"), ("zh", "core")
    return jax.shard_map(
        local,
        mesh=fine,
        in_specs=(P(seq, res, None), P(seq, res), P(), P(), P(), P()),
        out_specs=P(res, seq, None),
        check_vma=False,
    )
```

```python
import numpy as np

import jax
import jax.numpy as jnp
from jax import lax
from jax.experimental import pallas as pl
from jax.experimental.pallas import tpu as pltpu
from jax.sharding import Mesh
from jax.sharding import PartitionSpec as P

F32, BF16 = jnp.float32, jnp.bfloat16
SIZES = (8, 2, 4, 4, 2)
AXES = ("y", "zl", "x", "zh", "core")
S, I, C, WIDTH, PAIR = 64, 12, 256, 32, 128
ROWS = 208
NT = (((1,), (1,)), ((), ()))
VMEM = pl.BlockSpec(memory_space=pltpu.VMEM)
HBM = pl.BlockSpec(memory_space=pltpu.HBM)
SMEM = pl.BlockSpec(memory_space=pltpu.SMEM)


def one_hot(shape, match):
    row = lax.broadcasted_iota(jnp.int32, shape, 0)
    col = lax.broadcasted_iota(jnp.int32, shape, 1)
    return match(row, col).astype(F32).astype(BF16)


def dot(a, b, dims=(((1,), (0,)), ((), ()))):
    return lax.dot_general(a, b, dims, preferred_element_type=F32)


def project_kernel(
    x_in, m_in, wl_in, wr_in, offset_in, l_ref, r_ref, offset_ref, x_ref, m_ref, wl_ref, wr_ref, spread, sems
):
    copies = [
        pltpu.make_async_copy(source, target, sems.at[n])
        for n, (source, target) in enumerate(
            ((m_in, m_ref), (wl_in, wl_ref), (wr_in, wr_ref), (x_in, x_ref), (offset_in, offset_ref))
        )
    ]
    for copy in copies:
        copy.start()
    for copy in copies[:3]:
        copy.wait()
    mask = m_ref[...].astype(F32).astype(BF16)
    mask_twice = jnp.concatenate([mask, mask], axis=1)
    mask_rows = dot(one_hot((16, I), lambda r, t: r == t), mask_twice)
    mask_pairs = dot(one_hot((32, I), lambda r, t: r // 2 == t), mask_twice)
    mask_cols = dot(one_hot((S, S), lambda r, t: r == t), mask, NT)
    wl = dot(one_hot((128, WIDTH), lambda r, t: r % WIDTH == t), wl_ref[...]).astype(BF16)
    wr = dot(
        one_hot((WIDTH, WIDTH), lambda r, t: t == 2 * (r % 16) + r // 16), wr_ref[...]
    ).astype(BF16)
    copies[3].wait()
    low = lax.broadcasted_iota(jnp.int32, (8, 128), 1) < 64
    block = lax.broadcasted_iota(jnp.int32, (S, 128), 1) // WIDTH
    for g in range(I // 4):
        tile = None
        for k in range(4):
            i = 4 * g + k
            x = x_ref[i].astype(F32)
            centred = x - jnp.sum(x, axis=-1, keepdims=True) * (1.0 / C)
            variance = jnp.sum(centred * centred, axis=-1, keepdims=True) * (1.0 / C)
            xi = centred * lax.rsqrt(variance + 1e-05)
            high = xi.astype(BF16)
            rest = (xi - high.astype(F32)).astype(BF16)
            left = (dot(high, wl, NT) + dot(rest, wl, NT)) * mask_cols[:, i : i + 1]
            tile = left if k == 0 else jnp.where(block == k, left, tile)
            high2 = jnp.concatenate([high, high], axis=0)
            rest2 = jnp.concatenate([rest, rest], axis=0)
            right = (dot(wr, high2, NT) + dot(wr, rest2, NT)) * mask_rows[i : i + 1, :]
            for e in range(2):
                part = jnp.where(low, right[e * 16 : e * 16 + 8], right[e * 16 + 8 : e * 16 + 16])
                spread[pl.ds(2 * i + e, 8, stride=24), :] = part
        tile = tile.astype(BF16)
        for copy in range(4):
            l_ref[copy, g * S : (g + 1) * S, :] = tile
    for copy in range(4):
        l_ref[copy, 192:208, :] = mask_rows.astype(BF16)
    r_ref[0:192, :] = spread[...].astype(BF16)
    low16 = lax.broadcasted_iota(jnp.int32, (16, 128), 1) < 64
    r_ref[192:208, :] = jnp.where(low16, mask_pairs[0:16], mask_pairs[16:32]).astype(BF16)
    copies[4].wait()


SHIFT = ((4, 3), (1, 2), (0, 7), (6, 5))


def pair_kernel(at_ref, r_ref, w_ref, *refs):
    lm_refs, lo_refs, (out_ref, rt, rmask, lmask, z) = refs[:4], refs[4:8], refs[8:]
    zh, core, x = at_ref[0], at_ref[1], at_ref[2]
    low = lax.broadcasted_iota(jnp.int32, (ROWS, 128), 1) < 64
    low16 = lax.broadcasted_iota(jnp.int32, (16, 128), 1) < 64

    def piece(zl, t, c):
        step = (t - zh) & 3
        shift = jnp.int32(0)
        for n in range(4):
            for k in range(2):
                shift = jnp.where((step == n) & (c == k), SHIFT[n][k], shift)
        return r_ref[((2 * zh + core + shift) & 7) * 2 + zl].astype(F32)

    for zl in range(2):
        for t in range(4):
            a, b = piece(zl, t, core), piece(zl, t, 1 - core)
            first = jnp.where(low, a, pltpu.roll(b, 64, 1)).astype(BF16)
            second = jnp.where(low, pltpu.roll(a, 64, 1), b).astype(BF16)
            cols = slice(t * 128, t * 128 + 128)
            rt[zl, 0:192, cols] = first[0:192]
            rt[zl, 192:384, cols] = second[0:192]
            rmask[zl, 0:16, cols] = first[192:208]
            rmask[zl, 16:32, cols] = second[192:208]
    for k in range(4):
        for t in range(4):
            a = lm_refs[k][t, 192:208, :].astype(F32)
            b = lo_refs[k][t, 192:208, :].astype(F32)
            lmask[k * 16 : k * 16 + 16, t * 128 : t * 128 + 128] = jnp.where(low16, a, b).astype(BF16)
    scale = [1.0 / (dot(rmask[zl], lmask[...], NT) + 1.0) for zl in range(2)]

    lanes = lax.broadcasted_iota(jnp.int32, (24, 128), 1)
    half = lanes < 64
    even = (lanes // WIDTH) % 2 == 0
    for k in range(4):
        rhs = jnp.concatenate(
            [
                jnp.concatenate([ref[t, g * S : g * S + S, :] for g in range(3)], axis=1)
                for t in range(4)
                for ref in (lm_refs[k], lo_refs[k])
            ],
            axis=0,
        )
        for zl in range(2):
            outer = dot(rt[zl], rhs)
            left_rows = []
            for g in range(3):
                quads = [[], [], [], []]
                for q in range(4):
                    a = [
                        outer[(4 * q + n) * 24 : (4 * q + n) * 24 + 24, g * 128 : g * 128 + 128]
                        for n in range(4)
                    ]
                    a0 = jnp.where(half, a[0], pltpu.roll(a[2], 64, 1))
                    a1 = jnp.where(half, a[1], pltpu.roll(a[3], 64, 1))
                    a2 = jnp.where(half, pltpu.roll(a[0], 64, 1), a[2])
                    a3 = jnp.where(half, pltpu.roll(a[1], 64, 1), a[3])
                    quads[0].append(jnp.where(even, a0, pltpu.roll(a1, 32, 1)))
                    quads[1].append(jnp.where(even, pltpu.roll(a0, 96, 1), a1))
                    quads[2].append(jnp.where(even, a2, pltpu.roll(a3, 32, 1)))
                    quads[3].append(jnp.where(even, pltpu.roll(a2, 96, 1), a3))
                left_rows += [jnp.concatenate(quad, axis=1) for quad in quads]
            operand = jnp.concatenate(left_rows, axis=0).astype(BF16)
            wide = dot(operand, w_ref[...])
            for i in range(I):
                column = scale[zl][0:24, k * 16 + i : k * 16 + i + 1]
                for e in range(2):
                    z[e, i * 24 : i * 24 + 24, :] = (
                        wide[i * 24 : i * 24 + 24, e * 128 : e * 128 + 128] * column
                    )
            result = z[0, pl.ds(0, 144, stride=2), :] + z[1, pl.ds(1, 144, stride=2), :]
            out_ref[(x - k) & 3, zl] = result.astype(BF16)


def finish_kernel(pair_ref, offset_ref, out_ref):
    offset = offset_ref[...]
    for zl in range(2):
        for x1 in range(4):
            block = pair_ref[x1, zl].astype(F32) + offset
            at = (zl * 4 + x1) * I
            for i in range(I):
                out_ref[i, at : at + I, :] = block[i * I : i * I + I, :]


def swap(match):
    index = np.arange(int(np.prod(SIZES))).reshape(SIZES)
    return [(int(index[at]), int(index[match(*at)])) for at in np.ndindex(*SIZES)]


def shifted(y, zl, x, zh, c):
    return (y + SHIFT[(zh - y // 2) % 4][c]) % 8, zl, x, y // 2, y % 2


TRANSPOSE = swap(shifted)
ALONG_X = [swap(lambda y, zl, x, zh, c, k=k: (y, zl, (x + k) % 4, zh, c)) for k in range(4)]
OTHER_CORE = swap(lambda y, zl, x, zh, c: (y, zl, x, zh, 1 - c))


def spread_along(value, axis, count):
    return lax.all_to_all(
        jnp.broadcast_to(value[None], (count,) + value.shape), axis, 0, 0, tiled=True
    )


def call(kernel, out_shape, in_specs, scratch_shapes=(), vmem=48, flops=0, bytes_accessed=0):
    return pl.pallas_call(
        kernel,
        out_shape=out_shape,
        in_specs=in_specs,
        out_specs=jax.tree.map(lambda _: VMEM, out_shape),
        scratch_shapes=scratch_shapes,
        compiler_params=pltpu.CompilerParams(vmem_limit_bytes=vmem << 20),
        cost_estimate=pl.CostEstimate(
            flops=flops, bytes_accessed=bytes_accessed, transcendentals=0
        ),
    )


def local(x, m, wl, wr, w, offset):
    left, right, offset = call(
        project_kernel,
        [
            jax.ShapeDtypeStruct((4, ROWS, 128), BF16),
            jax.ShapeDtypeStruct((ROWS, 128), BF16),
            jax.ShapeDtypeStruct((1, PAIR), F32),
        ],
        [HBM] * 5,
        [
            pltpu.VMEM((I, S, C), BF16),
            pltpu.VMEM((I, S), jnp.int32),
            pltpu.VMEM((WIDTH, C), BF16),
            pltpu.VMEM((WIDTH, C), BF16),
            pltpu.VMEM((192, 128), F32),
            pltpu.SemaphoreType.DMA((5,)),
        ],
        vmem=60,
    )(x.transpose(1, 0, 2), m.T, wl.T, wr.T, offset.reshape(1, PAIR))
    w2 = w.reshape(WIDTH, 16, 2, PAIR).transpose(1, 0, 2, 3).reshape(512, 2 * PAIR)
    at = jnp.stack([lax.axis_index(name) for name in ("zh", "core", "x")]).astype(jnp.int32)

    right = lax.ppermute(right, AXES, TRANSPOSE)
    left = lax.all_to_all(left, "zh", 0, 0, tiled=True)
    right = spread_along(right, ("y", "zl"), 16)
    lefts = [left] + [lax.ppermute(left, AXES, ALONG_X[k]) for k in (1, 2, 3)]
    lefts += [lax.ppermute(left, AXES, OTHER_CORE) for left in lefts]

    pairs = call(
        pair_kernel,
        jax.ShapeDtypeStruct((4, 2, 144, 128), BF16),
        [SMEM] + [VMEM] * 10,
        [
            pltpu.VMEM((2, 384, 512), BF16),
            pltpu.VMEM((2, 32, 512), BF16),
            pltpu.VMEM((64, 512), BF16),
            pltpu.VMEM((2, 288, 128), F32),
        ],
        flops=3 << 30,
        bytes_accessed=4 << 20,
    )(at, right, w2, *lefts)
    pairs = lax.all_to_all(pairs, "x", 0, 0, tiled=True)
    return call(
        finish_kernel, jax.ShapeDtypeStruct((I, 96, PAIR), F32), [VMEM, VMEM]
    )(pairs, offset)


def solution(mesh):
    fine = Mesh(mesh.devices.reshape(SIZES), AXES)
    res, seq = ("y", "zl", "x"), ("zh", "core")
    return jax.shard_map(
        local,
        mesh=fine,
        in_specs=(P(seq, res, None), P(seq, res), P(), P(), P(), P()),
        out_specs=P(res, seq, None),
        check_vma=False,
    )
```

```python
import numpy as np

import jax
import jax.numpy as jnp
from jax import lax
from jax.experimental import pallas as pl
from jax.experimental.pallas import tpu as pltpu
from jax.sharding import Mesh
from jax.sharding import PartitionSpec as P

F32, BF16 = jnp.float32, jnp.bfloat16
SIZES = (8, 2, 4, 4, 2)
AXES = ("y", "zl", "x", "zh", "core")
S, I, C, WIDTH, PAIR = 64, 12, 256, 32, 128
ROWS = 208
NT = (((1,), (1,)), ((), ()))
VMEM = pl.BlockSpec(memory_space=pltpu.VMEM)
HBM = pl.BlockSpec(memory_space=pltpu.HBM)
SMEM = pl.BlockSpec(memory_space=pltpu.SMEM)


def one_hot(shape, match):
    row = lax.broadcasted_iota(jnp.int32, shape, 0)
    col = lax.broadcasted_iota(jnp.int32, shape, 1)
    return match(row, col).astype(F32).astype(BF16)


def dot(a, b, dims=(((1,), (0,)), ((), ()))):
    return lax.dot_general(a, b, dims, preferred_element_type=F32)


def project_kernel(
    x_in, m_in, wl_in, wr_in, offset_in, l_ref, r_ref, x_ref, m_ref, wl_ref, wr_ref, offset_ref, spread, sems
):
    pairs = [
        (x_in, x_ref), (m_in, m_ref), (wl_in, wl_ref), (wr_in, wr_ref), (offset_in, offset_ref)
    ]
    copies = [
        pltpu.make_async_copy(source, target, sems.at[n])
        for n, (source, target) in enumerate(pairs)
    ]
    for copy in copies:
        copy.start()
    for copy in copies:
        copy.wait()
    mask = m_ref[...].astype(F32).astype(BF16)
    mask_twice = jnp.concatenate([mask, mask], axis=1)
    mask_rows = dot(one_hot((16, I), lambda r, t: r == t), mask_twice)
    mask_pairs = dot(one_hot((32, I), lambda r, t: r // 2 == t), mask_twice)
    mask_cols = dot(one_hot((S, S), lambda r, t: r == t), mask, NT)
    wl = dot(one_hot((128, WIDTH), lambda r, t: r % WIDTH == t), wl_ref[...])
    wr = dot(
        one_hot((128, WIDTH), lambda r, t: t == 2 * (r % 16) + r % WIDTH // 16), wr_ref[...]
    )
    weights = jnp.concatenate([wl, wr], axis=0).astype(BF16)
    block = lax.broadcasted_iota(jnp.int32, (S, 256), 1) % 128 // WIDTH
    low = lax.broadcasted_iota(jnp.int32, (8, 128), 1) < 64
    for g in range(I // 4):
        x = x_ref[4 * g : 4 * g + 4].reshape(4 * S, C).astype(F32)
        centred = x - jnp.sum(x, axis=-1, keepdims=True) * (1.0 / C)
        variance = jnp.sum(centred * centred, axis=-1, keepdims=True) * (1.0 / C)
        normed = centred * lax.rsqrt(variance + 1e-05)
        high = normed.astype(BF16)
        rest = (normed - high.astype(F32)).astype(BF16)
        both = dot(high, weights, NT) + dot(rest, weights, NT)
        tile = None
        for k in range(4):
            i = 4 * g + k
            part = both[k * S : k * S + S] * mask_cols[:, i : i + 1]
            tile = part if k == 0 else jnp.where(block == k, part, tile)
        l_ref[0, g * S : (g + 1) * S, :] = tile[:, 0:128].astype(BF16)
        right = tile[:, 128:256]
        right = jnp.concatenate([right, right], axis=0).T
        for k in range(4):
            for e in range(2):
                row = k * WIDTH + e * 16
                part = jnp.where(low, right[row : row + 8], right[row + 8 : row + 16])
                spread[pl.ds(2 * (4 * g + k) + e, 8, stride=24), :] = part
    row = lax.broadcasted_iota(jnp.int32, (16, 128), 0)
    last, rest = mask_rows, offset_ref[...]
    for n in range(3):
        part = rest.astype(BF16).astype(F32)
        last = jnp.where(row == I + n, jnp.broadcast_to(part, (16, 128)), last)
        rest = rest - part
    l_ref[0, 192:208, :] = last.astype(BF16)
    r_ref[0:192, :] = spread[...].astype(BF16)
    low16 = lax.broadcasted_iota(jnp.int32, (16, 128), 1) < 64
    r_ref[192:208, :] = jnp.where(low16, mask_pairs[0:16], mask_pairs[16:32]).astype(BF16)


def placed(step, core):
    zl = (step >= 1) & (step <= 4)
    far = zl * (step - 1) + (1 - zl) * ((8 - step) & 7)
    return core * (3 - far) + (1 - core) * (4 + far), zl


def pair_kernel(at_ref, r_ref, w_ref, lm_ref, lo_ref, out_ref, offset_ref, rt, rmask, lmask, z):
    zh, core, x = at_ref[0], at_ref[1], at_ref[2]
    low = lax.broadcasted_iota(jnp.int32, (ROWS, 128), 1) < 64
    low16 = lax.broadcasted_iota(jnp.int32, (16, 128), 1) < 64

    def piece(zl, t, c):
        step = (2 * ((zh ^ (0, 2, 1, 3)[t]) - zh) + zl) & 7
        target = jnp.where((step >= 1) & (step <= 4), 1, 0)
        far = jnp.where(target == 1, step - 1, (8 - step) & 7)
        shift = jnp.where(c == 1, 3 - far, 4 + far)
        return r_ref[((2 * zh + core + shift) & 7) * 2 + target]

    for zl in range(2):
        for t in range(4):
            a, b = piece(zl, t, core), piece(zl, t, 1 - core)
            first = jnp.where(low, a, pltpu.roll(b, 64, 1))
            second = jnp.where(low, pltpu.roll(a, 64, 1), b)
            cols = slice(t * 128, t * 128 + 128)
            rt[zl, 0:192, cols] = first[0:192]
            rt[zl, 192:384, cols] = second[0:192]
            rmask[zl, 0:16, cols] = first[192:208]
            rmask[zl, 16:32, cols] = second[192:208]
    for k in range(4):
        for t in range(4):
            a, b = lm_ref[4 * k + t, 192:208, :], lo_ref[4 * k + t, 192:208, :]
            lmask[k * 16 : k * 16 + 16, t * 128 : t * 128 + 128] = jnp.where(low16, a, b)
    parts = lm_ref[0, 192:208, :].astype(F32)
    offset_ref[...] = parts[12:13] + parts[13:14] + parts[14:15]
    scale = jnp.concatenate(
        [1.0 / (dot(rmask[zl], lmask[...], NT)[0:24] + 1.0) for zl in range(2)], axis=0
    )

    lanes = lax.broadcasted_iota(jnp.int32, (48, 128), 1)
    half = lanes < 64
    even = (lanes // WIDTH) % 2 == 0
    for pair in range(2):
        rhs = jnp.concatenate(
            [
                jnp.concatenate(
                    [
                        ref[4 * k + t, g * S : g * S + S, :]
                        for k in (2 * pair, 2 * pair + 1)
                        for g in range(3)
                    ],
                    axis=1,
                )
                for t in range(4)
                for ref in (lm_ref, lo_ref)
            ],
            axis=0,
        )
        outer = [dot(rt[zl], rhs) for zl in range(2)]
        for n in range(2):
            left_rows = []
            for g in range(3 * n, 3 * n + 3):
                cols = slice(g * 128, g * 128 + 128)
                quads = [[], [], [], []]
                for q in range(4):
                    a = [
                        jnp.concatenate([o[e * 24 : e * 24 + 24, cols] for o in outer], axis=0)
                        .astype(BF16)
                        for e in range(4 * q, 4 * q + 4)
                    ]
                    a0 = jnp.where(half, a[0], pltpu.roll(a[2], 64, 1))
                    a1 = jnp.where(half, a[1], pltpu.roll(a[3], 64, 1))
                    a2 = jnp.where(half, pltpu.roll(a[0], 64, 1), a[2])
                    a3 = jnp.where(half, pltpu.roll(a[1], 64, 1), a[3])
                    quads[0].append(jnp.where(even, a0, pltpu.roll(a1, 32, 1)))
                    quads[1].append(jnp.where(even, pltpu.roll(a0, 96, 1), a1))
                    quads[2].append(jnp.where(even, a2, pltpu.roll(a3, 32, 1)))
                    quads[3].append(jnp.where(even, pltpu.roll(a2, 96, 1), a3))
                left_rows += [jnp.concatenate(quad, axis=1) for quad in quads]
            wide = dot(jnp.concatenate(left_rows, axis=0), w_ref[...])
            k = 2 * pair + n
            for i in range(I):
                column = scale[:, k * 16 + i : k * 16 + i + 1]
                for e in range(2):
                    z[e, i * 48 : i * 48 + 48, :] = (
                        wide[i * 48 : i * 48 + 48, e * 128 : e * 128 + 128] * column
                    )
            result = z[0, pl.ds(0, 288, stride=2), :] + z[1, pl.ds(1, 288, stride=2), :]
            out_ref[(x - k) & 3] = result.astype(BF16)


def finish_kernel(pair_ref, offset_ref, out_ref):
    offset = offset_ref[...]
    for x1 in range(4):
        block = pair_ref[x1].astype(F32) + offset
        for i in range(I):
            for zl in range(2):
                at, row = (zl * 4 + x1) * I, (2 * i + zl) * I
                out_ref[i, at : at + I, :] = block[row : row + I, :]


def swap(match):
    index = np.arange(int(np.prod(SIZES))).reshape(SIZES)
    return [(int(index[at]), int(index[match(*at)])) for at in np.ndindex(*SIZES)]


def shifted(y, zl, x, zh, c):
    shift, target = placed((2 * zh + zl - y // 2 * 2) % 8, c)
    return (y + shift) % 8, int(target), x, y // 2, y % 2


TRANSPOSE = swap(shifted)
ALONG_X = [swap(lambda y, zl, x, zh, c, k=k: (y, zl, (x + k) % 4, zh, c)) for k in range(4)]
ACROSS_ZH = [swap(lambda y, zl, x, zh, c, k=k: (y, zl, x, zh ^ k, c)) for k in range(4)]
OTHER_CORE = swap(lambda y, zl, x, zh, c: (y, zl, x, zh, 1 - c))


def spread_along(value, axis, count):
    return lax.all_to_all(
        jnp.broadcast_to(value[None], (count,) + value.shape), axis, 0, 0, tiled=True
    )


def call(kernel, out_shape, in_specs, scratch_shapes=(), vmem=48, flops=0, bytes_accessed=0):
    return pl.pallas_call(
        kernel,
        out_shape=out_shape,
        in_specs=in_specs,
        out_specs=jax.tree.map(lambda _: VMEM, out_shape),
        scratch_shapes=scratch_shapes,
        compiler_params=pltpu.CompilerParams(vmem_limit_bytes=vmem << 20),
        cost_estimate=pl.CostEstimate(
            flops=flops, bytes_accessed=bytes_accessed, transcendentals=0
        ),
    )


def local(x, m, wl, wr, w, offset):
    left, right = call(
        project_kernel,
        [
            jax.ShapeDtypeStruct((1, ROWS, 128), BF16),
            jax.ShapeDtypeStruct((ROWS, 128), BF16),
        ],
        [HBM] * 5,
        [
            pltpu.VMEM((I, S, C), BF16),
            pltpu.VMEM((I, S), jnp.int32),
            pltpu.VMEM((WIDTH, C), BF16),
            pltpu.VMEM((WIDTH, C), BF16),
            pltpu.VMEM((1, PAIR), F32),
            pltpu.VMEM((192, 128), F32),
            pltpu.SemaphoreType.DMA((5,)),
        ],
        vmem=60,
    )(x.transpose(1, 0, 2), m.T, wl.T, wr.T, offset.reshape(1, PAIR))
    w2 = w.reshape(WIDTH, 16, 2, PAIR).transpose(1, 0, 2, 3).reshape(512, 2 * PAIR)
    at = jnp.stack([lax.axis_index(name) for name in ("zh", "core", "x")]).astype(jnp.int32)

    right = lax.ppermute(right, AXES, TRANSPOSE)
    right = jnp.broadcast_to(right[None], (16, ROWS, 128))
    left = jnp.concatenate([left, lax.ppermute(left, AXES, ACROSS_ZH[2])])
    left = jnp.concatenate([left, lax.ppermute(left, AXES, ACROSS_ZH[1])])
    left = lax.optimization_barrier((left, right))[0]
    right = lax.all_to_all(right, ("y", "zl"), 0, 0, tiled=True)
    left = jnp.concatenate(
        [left] + [lax.ppermute(left, AXES, ALONG_X[k]) for k in (1, 2, 3)], axis=0
    )
    left_other = lax.ppermute(left, AXES, OTHER_CORE)

    pairs, offset = call(
        pair_kernel,
        [jax.ShapeDtypeStruct((4, 288, 128), BF16), jax.ShapeDtypeStruct((1, PAIR), F32)],
        [SMEM] + [VMEM] * 4,
        [
            pltpu.VMEM((2, 384, 512), BF16),
            pltpu.VMEM((2, 32, 512), BF16),
            pltpu.VMEM((64, 512), BF16),
            pltpu.VMEM((2, 576, 128), F32),
        ],
        flops=3 << 30,
        bytes_accessed=4 << 20,
    )(at, right, w2, left, left_other)
    pairs = lax.all_to_all(pairs, "x", 0, 0, tiled=True)
    return call(
        finish_kernel, jax.ShapeDtypeStruct((I, 96, PAIR), F32), [VMEM, VMEM]
    )(pairs, offset)


def solution(mesh):
    fine = Mesh(mesh.devices.reshape(SIZES), AXES)
    res, seq = ("y", "zl", "x"), ("zh", "core")
    return jax.shard_map(
        local,
        mesh=fine,
        in_specs=(P(seq, res, None), P(seq, res), P(), P(), P(), P()),
        out_specs=P(res, seq, None),
        check_vma=False,
    )
```

```python
import numpy as np

import jax
import jax.numpy as jnp
from jax import lax
from jax.experimental import pallas as pl
from jax.experimental.pallas import tpu as pltpu
from jax.sharding import Mesh
from jax.sharding import PartitionSpec as P

F32, BF16 = jnp.float32, jnp.bfloat16
SIZES = (8, 2, 4, 4, 2)
AXES = ("y", "zl", "x", "zh", "core")
S, I, C, WIDTH, PAIR = 64, 12, 256, 32, 128
ROWS = 208
NT = (((1,), (1,)), ((), ()))
VMEM = pl.BlockSpec(memory_space=pltpu.VMEM)
HBM = pl.BlockSpec(memory_space=pltpu.HBM)
SMEM = pl.BlockSpec(memory_space=pltpu.SMEM)


def one_hot(shape, match):
    row = lax.broadcasted_iota(jnp.int32, shape, 0)
    col = lax.broadcasted_iota(jnp.int32, shape, 1)
    return match(row, col).astype(F32).astype(BF16)


def dot(a, b, dims=(((1,), (0,)), ((), ()))):
    return lax.dot_general(a, b, dims, preferred_element_type=F32)


def project_kernel(
    x_in, m_in, wl_in, wr_in, offset_in, l_ref, r_ref, x_ref, m_ref, wl_ref, wr_ref, offset_ref, spread, sems
):
    pairs = [
        (x_in, x_ref), (m_in, m_ref), (wl_in, wl_ref), (wr_in, wr_ref), (offset_in, offset_ref)
    ]
    copies = [
        pltpu.make_async_copy(source, target, sems.at[n])
        for n, (source, target) in enumerate(pairs)
    ]
    for copy in copies:
        copy.start()
    for copy in copies:
        copy.wait()
    mask = m_ref[...].astype(F32).astype(BF16)
    mask_twice = jnp.concatenate([mask, mask], axis=1)
    mask_rows = dot(one_hot((16, I), lambda r, t: r == t), mask_twice)
    mask_pairs = dot(one_hot((32, I), lambda r, t: r // 2 == t), mask_twice)
    mask_cols = dot(one_hot((S, S), lambda r, t: r == t), mask, NT)
    wl = dot(one_hot((128, WIDTH), lambda r, t: r % WIDTH == t), wl_ref[...])
    wr = dot(
        one_hot((128, WIDTH), lambda r, t: t == 2 * (r % 16) + r % WIDTH // 16), wr_ref[...]
    )
    weights = jnp.concatenate([wl, wr], axis=0).astype(BF16)
    block = lax.broadcasted_iota(jnp.int32, (S, 256), 1) % 128 // WIDTH
    low = lax.broadcasted_iota(jnp.int32, (8, 128), 1) < 64
    for g in range(I // 4):
        x = x_ref[4 * g : 4 * g + 4].reshape(4 * S, C).astype(F32)
        centred = x - jnp.sum(x, axis=-1, keepdims=True) * (1.0 / C)
        variance = jnp.sum(centred * centred, axis=-1, keepdims=True) * (1.0 / C)
        normed = centred * lax.rsqrt(variance + 1e-05)
        high = normed.astype(BF16)
        rest = (normed - high.astype(F32)).astype(BF16)
        both = dot(high, weights, NT) + dot(rest, weights, NT)
        tile = None
        for k in range(4):
            i = 4 * g + k
            part = both[k * S : k * S + S] * mask_cols[:, i : i + 1]
            tile = part if k == 0 else jnp.where(block == k, part, tile)
        l_ref[0, g * S : (g + 1) * S, :] = tile[:, 0:128].astype(BF16)
        right = tile[:, 128:256]
        right = jnp.concatenate([right, right], axis=0).T
        for k in range(4):
            for e in range(2):
                row = k * WIDTH + e * 16
                part = jnp.where(low, right[row : row + 8], right[row + 8 : row + 16])
                spread[pl.ds(2 * (4 * g + k) + e, 8, stride=24), :] = part
    row = lax.broadcasted_iota(jnp.int32, (16, 128), 0)
    last, rest = mask_rows, offset_ref[...]
    for n in range(3):
        part = rest.astype(BF16).astype(F32)
        last = jnp.where(row == I + n, jnp.broadcast_to(part, (16, 128)), last)
        rest = rest - part
    l_ref[0, 192:208, :] = last.astype(BF16)
    r_ref[0:192, :] = spread[...].astype(BF16)
    low16 = lax.broadcasted_iota(jnp.int32, (16, 128), 1) < 64
    r_ref[192:208, :] = jnp.where(low16, mask_pairs[0:16], mask_pairs[16:32]).astype(BF16)


def placed(step, core):
    zl = (step >= 1) & (step <= 4)
    far = zl * (step - 1) + (1 - zl) * ((8 - step) & 7)
    return core * (3 - far) + (1 - core) * (4 + far), zl


def pair_kernel(at_ref, r_ref, w_ref, lm_ref, lo_ref, out_ref, offset_ref, rt, rmask, lmask, z):
    zh, core, x = at_ref[0], at_ref[1], at_ref[2]
    low = lax.broadcasted_iota(jnp.int32, (ROWS, 128), 1) < 64
    low16 = lax.broadcasted_iota(jnp.int32, (16, 128), 1) < 64

    def piece(zl, t, c):
        step = (2 * ((zh ^ (0, 2, 1, 3)[t]) - zh) + zl) & 7
        target = jnp.where((step >= 1) & (step <= 4), 1, 0)
        far = jnp.where(target == 1, step - 1, (8 - step) & 7)
        shift = jnp.where(c == 1, 3 - far, 4 + far)
        return r_ref[((2 * zh + core + shift) & 7) * 2 + target]

    for zl in range(2):
        for t in range(4):
            a, b = piece(zl, t, core), piece(zl, t, 1 - core)
            first = jnp.where(low, a, pltpu.roll(b, 64, 1))
            second = jnp.where(low, pltpu.roll(a, 64, 1), b)
            cols = slice(t * 128, t * 128 + 128)
            rt[zl, 0:192, cols] = first[0:192]
            rt[zl, 192:384, cols] = second[0:192]
            rmask[zl, 0:16, cols] = first[192:208]
            rmask[zl, 16:32, cols] = second[192:208]
    for k in range(4):
        for t in range(4):
            a, b = lm_ref[4 * k + t, 192:208, :], lo_ref[4 * k + t, 192:208, :]
            lmask[k * 16 : k * 16 + 16, t * 128 : t * 128 + 128] = jnp.where(low16, a, b)
    parts = lm_ref[0, 192:208, :].astype(F32)
    offset_ref[...] = parts[12:13] + parts[13:14] + parts[14:15]
    scale = jnp.concatenate(
        [1.0 / (dot(rmask[zl], lmask[...], NT)[0:24] + 1.0) for zl in range(2)], axis=0
    )

    lanes = lax.broadcasted_iota(jnp.int32, (48, 128), 1)
    half = lanes < 64
    even = (lanes // WIDTH) % 2 == 0
    for pair in range(2):
        rhs = jnp.concatenate(
            [
                jnp.concatenate(
                    [
                        ref[4 * k + t, g * S : g * S + S, :]
                        for k in (2 * pair, 2 * pair + 1)
                        for g in range(3)
                    ],
                    axis=1,
                )
                for t in range(4)
                for ref in (lm_ref, lo_ref)
            ],
            axis=0,
        )
        outer = [dot(rt[zl], rhs) for zl in range(2)]
        for n in range(2):
            left_rows = []
            for g in range(3 * n, 3 * n + 3):
                cols = slice(g * 128, g * 128 + 128)
                quads = [[], [], [], []]
                for q in range(4):
                    a = [
                        jnp.concatenate([o[e * 24 : e * 24 + 24, cols] for o in outer], axis=0)
                        .astype(BF16)
                        for e in range(4 * q, 4 * q + 4)
                    ]
                    a0 = jnp.where(half, a[0], pltpu.roll(a[2], 64, 1))
                    a1 = jnp.where(half, a[1], pltpu.roll(a[3], 64, 1))
                    a2 = jnp.where(half, pltpu.roll(a[0], 64, 1), a[2])
                    a3 = jnp.where(half, pltpu.roll(a[1], 64, 1), a[3])
                    quads[0].append(jnp.where(even, a0, pltpu.roll(a1, 32, 1)))
                    quads[1].append(jnp.where(even, pltpu.roll(a0, 96, 1), a1))
                    quads[2].append(jnp.where(even, a2, pltpu.roll(a3, 32, 1)))
                    quads[3].append(jnp.where(even, pltpu.roll(a2, 96, 1), a3))
                left_rows += [jnp.concatenate(quad, axis=1) for quad in quads]
            wide = dot(jnp.concatenate(left_rows, axis=0), w_ref[...])
            k = 2 * pair + n
            for i in range(I):
                column = scale[:, k * 16 + i : k * 16 + i + 1]
                for e in range(2):
                    z[e, i * 48 : i * 48 + 48, :] = (
                        wide[i * 48 : i * 48 + 48, e * 128 : e * 128 + 128] * column
                    )
            result = z[0, pl.ds(0, 288, stride=2), :] + z[1, pl.ds(1, 288, stride=2), :]
            out_ref[(x - k) & 3] = result.astype(BF16)


def finish_kernel(pair_ref, offset_ref, out_ref):
    offset = offset_ref[...]
    for x1 in range(4):
        block = pair_ref[x1].astype(F32) + offset
        for i in range(I):
            for zl in range(2):
                at, row = (zl * 4 + x1) * I, (2 * i + zl) * I
                out_ref[i, at : at + I, :] = block[row : row + I, :]


def swap(match):
    index = np.arange(int(np.prod(SIZES))).reshape(SIZES)
    return [(int(index[at]), int(index[match(*at)])) for at in np.ndindex(*SIZES)]


def shifted(y, zl, x, zh, c):
    shift, target = placed((2 * zh + zl - y // 2 * 2) % 8, c)
    return (y + shift) % 8, int(target), x, y // 2, y % 2


TRANSPOSE = swap(shifted)
ALONG_X = [swap(lambda y, zl, x, zh, c, k=k: (y, zl, (x + k) % 4, zh, c)) for k in range(4)]
ACROSS_ZH = [swap(lambda y, zl, x, zh, c, k=k: (y, zl, x, zh ^ k, c)) for k in range(4)]
OTHER_CORE = swap(lambda y, zl, x, zh, c: (y, zl, x, zh, 1 - c))


def spread_along(value, axis, count):
    return lax.all_to_all(
        jnp.broadcast_to(value[None], (count,) + value.shape), axis, 0, 0, tiled=True
    )


def call(kernel, out_shape, in_specs, scratch_shapes=(), vmem=48, flops=0, bytes_accessed=0):
    return pl.pallas_call(
        kernel,
        out_shape=out_shape,
        in_specs=in_specs,
        out_specs=jax.tree.map(lambda _: VMEM, out_shape),
        scratch_shapes=scratch_shapes,
        compiler_params=pltpu.CompilerParams(vmem_limit_bytes=vmem << 20),
        cost_estimate=pl.CostEstimate(
            flops=flops, bytes_accessed=bytes_accessed, transcendentals=0
        ),
    )


def local(x, m, wl, wr, w, offset):
    left, right = call(
        project_kernel,
        [
            jax.ShapeDtypeStruct((1, ROWS, 128), BF16),
            jax.ShapeDtypeStruct((ROWS, 128), BF16),
        ],
        [HBM] * 5,
        [
            pltpu.VMEM((I, S, C), BF16),
            pltpu.VMEM((I, S), jnp.int32),
            pltpu.VMEM((WIDTH, C), BF16),
            pltpu.VMEM((WIDTH, C), BF16),
            pltpu.VMEM((1, PAIR), F32),
            pltpu.VMEM((192, 128), F32),
            pltpu.SemaphoreType.DMA((5,)),
        ],
        vmem=60,
    )(x.transpose(1, 0, 2), m.T, wl.T, wr.T, offset.reshape(1, PAIR))
    w2 = w.reshape(WIDTH, 16, 2, PAIR).transpose(1, 0, 2, 3).reshape(512, 2 * PAIR)
    at = jnp.stack([lax.axis_index(name) for name in ("zh", "core", "x")]).astype(jnp.int32)

    right = lax.ppermute(right, AXES, TRANSPOSE)
    right = jnp.broadcast_to(right[None], (16, ROWS, 128))
    left = lax.optimization_barrier(
        jnp.concatenate([left, lax.ppermute(left, AXES, ACROSS_ZH[2])])
    )
    left = jnp.concatenate([left, lax.ppermute(left, AXES, ACROSS_ZH[1])])
    left = lax.optimization_barrier((left, right))[0]
    right = lax.all_to_all(right, ("y", "zl"), 0, 0, tiled=True)
    left = jnp.concatenate(
        [left] + [lax.ppermute(left, AXES, ALONG_X[k]) for k in (1, 2, 3)], axis=0
    )
    left_other = lax.ppermute(left, AXES, OTHER_CORE)

    pairs, offset = call(
        pair_kernel,
        [jax.ShapeDtypeStruct((4, 288, 128), BF16), jax.ShapeDtypeStruct((1, PAIR), F32)],
        [SMEM] + [VMEM] * 4,
        [
            pltpu.VMEM((2, 384, 512), BF16),
            pltpu.VMEM((2, 32, 512), BF16),
            pltpu.VMEM((64, 512), BF16),
            pltpu.VMEM((2, 576, 128), F32),
        ],
        flops=3 << 30,
        bytes_accessed=4 << 20,
    )(at, right, w2, left, left_other)
    pairs = lax.all_to_all(pairs, "x", 0, 0, tiled=True)
    return call(
        finish_kernel, jax.ShapeDtypeStruct((I, 96, PAIR), F32), [VMEM, VMEM]
    )(pairs, offset)


def solution(mesh):
    fine = Mesh(mesh.devices.reshape(SIZES), AXES)
    res, seq = ("y", "zl", "x"), ("zh", "core")
    return jax.shard_map(
        local,
        mesh=fine,
        in_specs=(P(seq, res, None), P(seq, res), P(), P(), P(), P()),
        out_specs=P(res, seq, None),
        check_vma=False,
    )
```

```python
import numpy as np

import jax
import jax.numpy as jnp
from jax import lax
from jax.experimental import pallas as pl
from jax.experimental.pallas import tpu as pltpu
from jax.sharding import Mesh
from jax.sharding import PartitionSpec as P

F32, BF16 = jnp.float32, jnp.bfloat16
SIZES = (8, 2, 4, 4, 2)
AXES = ("y", "zl", "x", "zh", "core")
S, I, C, WIDTH, PAIR = 64, 12, 256, 32, 128
ROWS = 208
NT = (((1,), (1,)), ((), ()))
VMEM = pl.BlockSpec(memory_space=pltpu.VMEM)
HBM = pl.BlockSpec(memory_space=pltpu.HBM)
SMEM = pl.BlockSpec(memory_space=pltpu.SMEM)


def one_hot(shape, match):
    row = lax.broadcasted_iota(jnp.int32, shape, 0)
    col = lax.broadcasted_iota(jnp.int32, shape, 1)
    return match(row, col).astype(F32).astype(BF16)


def dot(a, b, dims=(((1,), (0,)), ((), ()))):
    return lax.dot_general(a, b, dims, preferred_element_type=F32)


def project_kernel(
    x_in, m_in, wl_in, wr_in, offset_in, l_ref, r_ref, x_ref, m_ref, wl_ref, wr_ref, offset_ref, spread, sems
):
    pairs = [
        (x_in, x_ref), (m_in, m_ref), (wl_in, wl_ref), (wr_in, wr_ref), (offset_in, offset_ref)
    ]
    copies = [
        pltpu.make_async_copy(source, target, sems.at[n])
        for n, (source, target) in enumerate(pairs)
    ]
    for copy in copies:
        copy.start()
    for copy in copies:
        copy.wait()
    mask = m_ref[...].astype(F32).astype(BF16)
    mask_twice = jnp.concatenate([mask, mask], axis=1)
    mask_rows = dot(one_hot((16, I), lambda r, t: r == t), mask_twice)
    mask_pairs = dot(one_hot((32, I), lambda r, t: r // 2 == t), mask_twice)
    mask_cols = dot(one_hot((S, S), lambda r, t: r == t), mask, NT)
    wl = dot(one_hot((128, WIDTH), lambda r, t: r % WIDTH == t), wl_ref[...])
    wr = dot(
        one_hot((128, WIDTH), lambda r, t: t == 2 * (r % 16) + r % WIDTH // 16), wr_ref[...]
    )
    weights = jnp.concatenate([wl, wr], axis=0).astype(BF16)
    block = lax.broadcasted_iota(jnp.int32, (S, 256), 1) % 128 // WIDTH
    low = lax.broadcasted_iota(jnp.int32, (8, 128), 1) < 64
    for g in range(I // 4):
        x = x_ref[4 * g : 4 * g + 4].reshape(4 * S, C).astype(F32)
        centred = x - jnp.sum(x, axis=-1, keepdims=True) * (1.0 / C)
        variance = jnp.sum(centred * centred, axis=-1, keepdims=True) * (1.0 / C)
        normed = centred * lax.rsqrt(variance + 1e-05)
        high = normed.astype(BF16)
        rest = (normed - high.astype(F32)).astype(BF16)
        both = dot(high, weights, NT) + dot(rest, weights, NT)
        tile = None
        for k in range(4):
            i = 4 * g + k
            part = both[k * S : k * S + S] * mask_cols[:, i : i + 1]
            tile = part if k == 0 else jnp.where(block == k, part, tile)
        l_ref[0, g * S : (g + 1) * S, :] = tile[:, 0:128].astype(BF16)
        right = tile[:, 128:256]
        right = jnp.concatenate([right, right], axis=0).T
        for k in range(4):
            for e in range(2):
                row = k * WIDTH + e * 16
                part = jnp.where(low, right[row : row + 8], right[row + 8 : row + 16])
                spread[pl.ds(2 * (4 * g + k) + e, 8, stride=24), :] = part
    row = lax.broadcasted_iota(jnp.int32, (16, 128), 0)
    last, rest = mask_rows, offset_ref[...]
    for n in range(3):
        part = rest.astype(BF16).astype(F32)
        last = jnp.where(row == I + n, jnp.broadcast_to(part, (16, 128)), last)
        rest = rest - part
    l_ref[0, 192:208, :] = last.astype(BF16)
    r_ref[0:192, :] = spread[...].astype(BF16)
    low16 = lax.broadcasted_iota(jnp.int32, (16, 128), 1) < 64
    r_ref[192:208, :] = jnp.where(low16, mask_pairs[0:16], mask_pairs[16:32]).astype(BF16)


def placed(step, core):
    zl = (step >= 1) & (step <= 4)
    far = zl * (step - 1) + (1 - zl) * ((8 - step) & 7)
    return core * (3 - far) + (1 - core) * (4 + far), zl


def pair_kernel(at_ref, r_ref, w_ref, lm_ref, lo_ref, out_ref, offset_ref, rt, rmask, lmask, z):
    zh, core, x = at_ref[0], at_ref[1], at_ref[2]
    low = lax.broadcasted_iota(jnp.int32, (ROWS, 128), 1) < 64
    low16 = lax.broadcasted_iota(jnp.int32, (16, 128), 1) < 64

    def piece(zl, t, c):
        step = (2 * ((zh ^ (0, 2, 1, 3)[t]) - zh) + zl) & 7
        target = jnp.where((step >= 1) & (step <= 4), 1, 0)
        far = jnp.where(target == 1, step - 1, (8 - step) & 7)
        shift = jnp.where(c == 1, 3 - far, 4 + far)
        return r_ref[((2 * zh + core + shift) & 7) * 2 + target]

    for zl in range(2):
        for t in range(4):
            a, b = piece(zl, t, core), piece(zl, t, 1 - core)
            first = jnp.where(low, a, pltpu.roll(b, 64, 1))
            second = jnp.where(low, pltpu.roll(a, 64, 1), b)
            cols = slice(t * 128, t * 128 + 128)
            rt[zl, 0:192, cols] = first[0:192]
            rt[zl, 192:384, cols] = second[0:192]
            rmask[zl, 0:16, cols] = first[192:208]
            rmask[zl, 16:32, cols] = second[192:208]
    for k in range(4):
        for t in range(4):
            a, b = lm_ref[4 * k + t, 192:208, :], lo_ref[4 * k + t, 192:208, :]
            lmask[k * 16 : k * 16 + 16, t * 128 : t * 128 + 128] = jnp.where(low16, a, b)
    parts = lm_ref[0, 192:208, :].astype(F32)
    offset_ref[...] = parts[12:13] + parts[13:14] + parts[14:15]
    scale = jnp.concatenate(
        [1.0 / (dot(rmask[zl], lmask[...], NT)[0:24] + 1.0) for zl in range(2)], axis=0
    )

    lanes = lax.broadcasted_iota(jnp.int32, (48, 128), 1)
    half = lanes < 64
    even = (lanes // WIDTH) % 2 == 0
    for pair in range(2):
        rhs = jnp.concatenate(
            [
                jnp.concatenate(
                    [
                        ref[4 * k + t, g * S : g * S + S, :]
                        for k in (2 * pair, 2 * pair + 1)
                        for g in range(3)
                    ],
                    axis=1,
                )
                for t in range(4)
                for ref in (lm_ref, lo_ref)
            ],
            axis=0,
        )
        outer = [dot(rt[zl], rhs) for zl in range(2)]
        for n in range(2):
            left_rows = []
            for g in range(3 * n, 3 * n + 3):
                cols = slice(g * 128, g * 128 + 128)
                quads = [[], [], [], []]
                for q in range(4):
                    a = [
                        jnp.concatenate([o[e * 24 : e * 24 + 24, cols] for o in outer], axis=0)
                        .astype(BF16)
                        for e in range(4 * q, 4 * q + 4)
                    ]
                    a0 = jnp.where(half, a[0], pltpu.roll(a[2], 64, 1))
                    a1 = jnp.where(half, a[1], pltpu.roll(a[3], 64, 1))
                    a2 = jnp.where(half, pltpu.roll(a[0], 64, 1), a[2])
                    a3 = jnp.where(half, pltpu.roll(a[1], 64, 1), a[3])
                    quads[0].append(jnp.where(even, a0, pltpu.roll(a1, 32, 1)))
                    quads[1].append(jnp.where(even, pltpu.roll(a0, 96, 1), a1))
                    quads[2].append(jnp.where(even, a2, pltpu.roll(a3, 32, 1)))
                    quads[3].append(jnp.where(even, pltpu.roll(a2, 96, 1), a3))
                left_rows += [jnp.concatenate(quad, axis=1) for quad in quads]
            wide = dot(jnp.concatenate(left_rows, axis=0), w_ref[...])
            k = 2 * pair + n
            for i in range(I):
                column = scale[:, k * 16 + i : k * 16 + i + 1]
                for e in range(2):
                    z[e, i * 48 : i * 48 + 48, :] = (
                        wide[i * 48 : i * 48 + 48, e * 128 : e * 128 + 128] * column
                    )
            result = z[0, pl.ds(0, 288, stride=2), :] + z[1, pl.ds(1, 288, stride=2), :]
            out_ref[(x - k) & 3] = result.astype(BF16)


def finish_kernel(pair_ref, offset_ref, out_ref):
    offset = offset_ref[...]
    for x1 in range(4):
        block = pair_ref[x1].astype(F32) + offset
        for i in range(I):
            for zl in range(2):
                at, row = (zl * 4 + x1) * I, (2 * i + zl) * I
                out_ref[i, at : at + I, :] = block[row : row + I, :]


def swap(match):
    index = np.arange(int(np.prod(SIZES))).reshape(SIZES)
    return [(int(index[at]), int(index[match(*at)])) for at in np.ndindex(*SIZES)]


def shifted(y, zl, x, zh, c):
    shift, target = placed((2 * zh + zl - y // 2 * 2) % 8, c)
    return (y + shift) % 8, int(target), x, y // 2, y % 2


TRANSPOSE = swap(shifted)
ALONG_X = [swap(lambda y, zl, x, zh, c, k=k: (y, zl, (x + k) % 4, zh, c)) for k in range(4)]
ACROSS_ZH = [swap(lambda y, zl, x, zh, c, k=k: (y, zl, x, zh ^ k, c)) for k in range(4)]
OTHER_CORE = swap(lambda y, zl, x, zh, c: (y, zl, x, zh, 1 - c))


def spread_along(value, axis, count):
    return lax.all_to_all(
        jnp.broadcast_to(value[None], (count,) + value.shape), axis, 0, 0, tiled=True
    )


def stay(value):
    return pltpu.with_memory_space_constraint(value, pltpu.HBM)


def call(kernel, out_shape, in_specs, scratch_shapes=(), vmem=48, flops=0, bytes_accessed=0):
    return pl.pallas_call(
        kernel,
        out_shape=out_shape,
        in_specs=in_specs,
        out_specs=jax.tree.map(lambda _: VMEM, out_shape),
        scratch_shapes=scratch_shapes,
        compiler_params=pltpu.CompilerParams(vmem_limit_bytes=vmem << 20),
        cost_estimate=pl.CostEstimate(
            flops=flops, bytes_accessed=bytes_accessed, transcendentals=0
        ),
    )


def local(x, m, wl, wr, w, offset):
    left, right = call(
        project_kernel,
        [
            jax.ShapeDtypeStruct((1, ROWS, 128), BF16),
            jax.ShapeDtypeStruct((ROWS, 128), BF16),
        ],
        [HBM] * 5,
        [
            pltpu.VMEM((I, S, C), BF16),
            pltpu.VMEM((I, S), jnp.int32),
            pltpu.VMEM((WIDTH, C), BF16),
            pltpu.VMEM((WIDTH, C), BF16),
            pltpu.VMEM((1, PAIR), F32),
            pltpu.VMEM((192, 128), F32),
            pltpu.SemaphoreType.DMA((5,)),
        ],
    )(*map(stay, (x.transpose(1, 0, 2), m.T, wl.T, wr.T, offset.reshape(1, PAIR))))
    w2 = w.reshape(WIDTH, 16, 2, PAIR).transpose(1, 0, 2, 3).reshape(512, 2 * PAIR)
    at = jnp.stack([lax.axis_index(name) for name in ("zh", "core", "x")]).astype(jnp.int32)

    right = lax.ppermute(right, AXES, TRANSPOSE)
    right = jnp.broadcast_to(right[None], (16, ROWS, 128))
    left = lax.optimization_barrier(
        jnp.concatenate([left, lax.ppermute(left, AXES, ACROSS_ZH[2])])
    )
    left = jnp.concatenate([left, lax.ppermute(left, AXES, ACROSS_ZH[1])])
    left = lax.optimization_barrier((left, right))[0]
    right = lax.all_to_all(right, ("y", "zl"), 0, 0, tiled=True)
    along = {k: lax.ppermute(left, AXES, ALONG_X[k]) for k in (2, 3, 1)}
    left = jnp.concatenate([left, along[1], along[2], along[3]], axis=0)
    left_other = lax.ppermute(left, AXES, OTHER_CORE)

    pairs, offset = call(
        pair_kernel,
        [jax.ShapeDtypeStruct((4, 288, 128), BF16), jax.ShapeDtypeStruct((1, PAIR), F32)],
        [SMEM] + [VMEM] * 4,
        [
            pltpu.VMEM((2, 384, 512), BF16),
            pltpu.VMEM((2, 32, 512), BF16),
            pltpu.VMEM((64, 512), BF16),
            pltpu.VMEM((2, 576, 128), F32),
        ],
        flops=3 << 30,
        bytes_accessed=4 << 20,
    )(at, right, w2, left, left_other)
    pairs = lax.all_to_all(pairs, "x", 0, 0, tiled=True)
    return call(
        finish_kernel, jax.ShapeDtypeStruct((I, 96, PAIR), F32), [VMEM, VMEM]
    )(pairs, offset)


def solution(mesh):
    fine = Mesh(mesh.devices.reshape(SIZES), AXES)
    res, seq = ("y", "zl", "x"), ("zh", "core")
    return jax.shard_map(
        local,
        mesh=fine,
        in_specs=(P(seq, res, None), P(seq, res), P(), P(), P(), P()),
        out_specs=P(res, seq, None),
        check_vma=False,
    )
```

```python
import numpy as np

import jax
import jax.numpy as jnp
from jax import lax
from jax.experimental import pallas as pl
from jax.experimental.pallas import tpu as pltpu
from jax.sharding import Mesh
from jax.sharding import PartitionSpec as P

F32, BF16 = jnp.float32, jnp.bfloat16
SIZES = (8, 2, 4, 4, 2)
AXES = ("y", "zl", "x", "zh", "core")
S, I, C, WIDTH, PAIR = 64, 12, 256, 32, 128
ROWS = 208
NT = (((1,), (1,)), ((), ()))
VMEM = pl.BlockSpec(memory_space=pltpu.VMEM)
HBM = pl.BlockSpec(memory_space=pltpu.HBM)
SMEM = pl.BlockSpec(memory_space=pltpu.SMEM)


def one_hot(shape, match):
    row = lax.broadcasted_iota(jnp.int32, shape, 0)
    col = lax.broadcasted_iota(jnp.int32, shape, 1)
    return match(row, col).astype(F32).astype(BF16)


def dot(a, b, dims=(((1,), (0,)), ((), ()))):
    return lax.dot_general(a, b, dims, preferred_element_type=F32)


def project_kernel(
    x_in, m_in, wl_in, wr_in, offset_in, l_ref, r_ref, x_ref, m_ref, wl_ref, wr_ref, offset_ref, spread, sems
):
    pairs = [
        (x_in, x_ref), (m_in, m_ref), (wl_in, wl_ref), (wr_in, wr_ref), (offset_in, offset_ref)
    ]
    copies = [
        pltpu.make_async_copy(source, target, sems.at[n])
        for n, (source, target) in enumerate(pairs)
    ]
    for copy in copies:
        copy.start()
    for copy in copies:
        copy.wait()
    mask = m_ref[...].astype(F32).astype(BF16)
    mask_twice = jnp.concatenate([mask, mask], axis=1)
    mask_rows = dot(one_hot((16, I), lambda r, t: r == t), mask_twice)
    mask_pairs = dot(one_hot((32, I), lambda r, t: r // 2 == t), mask_twice)
    mask_cols = dot(one_hot((S, S), lambda r, t: r == t), mask, NT)
    wl = dot(one_hot((128, WIDTH), lambda r, t: r % WIDTH == t), wl_ref[...])
    wr = dot(
        one_hot((128, WIDTH), lambda r, t: t == 2 * (r % 16) + r % WIDTH // 16), wr_ref[...]
    )
    weights = jnp.concatenate([wl, wr], axis=0).astype(BF16)
    block = lax.broadcasted_iota(jnp.int32, (S, 256), 1) % 128 // WIDTH
    low = lax.broadcasted_iota(jnp.int32, (8, 128), 1) < 64
    for g in range(I // 4):
        x = x_ref[4 * g : 4 * g + 4].reshape(4 * S, C).astype(F32)
        centred = x - jnp.sum(x, axis=-1, keepdims=True) * (1.0 / C)
        variance = jnp.sum(centred * centred, axis=-1, keepdims=True) * (1.0 / C)
        normed = centred * lax.rsqrt(variance + 1e-05)
        high = normed.astype(BF16)
        rest = (normed - high.astype(F32)).astype(BF16)
        both = dot(high, weights, NT) + dot(rest, weights, NT)
        tile = None
        for k in range(4):
            i = 4 * g + k
            part = both[k * S : k * S + S] * mask_cols[:, i : i + 1]
            tile = part if k == 0 else jnp.where(block == k, part, tile)
        l_ref[0, g * S : (g + 1) * S, :] = tile[:, 0:128].astype(BF16)
        right = tile[:, 128:256]
        right = jnp.concatenate([right, right], axis=0).T
        for k in range(4):
            for e in range(2):
                row = k * WIDTH + e * 16
                part = jnp.where(low, right[row : row + 8], right[row + 8 : row + 16])
                spread[pl.ds(2 * (4 * g + k) + e, 8, stride=24), :] = part
    row = lax.broadcasted_iota(jnp.int32, (16, 128), 0)
    last, rest = mask_rows, offset_ref[...]
    for n in range(3):
        part = rest.astype(BF16).astype(F32)
        last = jnp.where(row == I + n, jnp.broadcast_to(part, (16, 128)), last)
        rest = rest - part
    l_ref[0, 192:208, :] = last.astype(BF16)
    r_ref[0:192, :] = spread[...].astype(BF16)
    low16 = lax.broadcasted_iota(jnp.int32, (16, 128), 1) < 64
    r_ref[192:208, :] = jnp.where(low16, mask_pairs[0:16], mask_pairs[16:32]).astype(BF16)


def placed(step, core):
    zl = (step >= 1) & (step <= 4)
    far = zl * (step - 1) + (1 - zl) * ((8 - step) & 7)
    return core * (3 - far) + (1 - core) * (4 + far), zl


def pair_kernel(at_ref, r_ref, w_ref, lm_ref, lo_ref, out_ref, offset_ref, rt, rmask, lmask, z):
    zh, core, x = at_ref[0], at_ref[1], at_ref[2]
    low = lax.broadcasted_iota(jnp.int32, (ROWS, 128), 1) < 64
    low16 = lax.broadcasted_iota(jnp.int32, (16, 128), 1) < 64

    def piece(zl, t, c):
        step = (2 * ((zh ^ (0, 2, 1, 3)[t]) - zh) + zl) & 7
        target = jnp.where((step >= 1) & (step <= 4), 1, 0)
        far = jnp.where(target == 1, step - 1, (8 - step) & 7)
        shift = jnp.where(c == 1, 3 - far, 4 + far)
        return r_ref[((2 * zh + core + shift) & 7) * 2 + target]

    for zl in range(2):
        for t in range(4):
            a, b = piece(zl, t, core), piece(zl, t, 1 - core)
            first = jnp.where(low, a, pltpu.roll(b, 64, 1))
            second = jnp.where(low, pltpu.roll(a, 64, 1), b)
            cols = slice(t * 128, t * 128 + 128)
            rt[zl, 0:192, cols] = first[0:192]
            rt[zl, 192:384, cols] = second[0:192]
            rmask[zl, 0:16, cols] = first[192:208]
            rmask[zl, 16:32, cols] = second[192:208]
    for k in range(4):
        for t in range(4):
            a, b = lm_ref[4 * k + t, 192:208, :], lo_ref[4 * k + t, 192:208, :]
            lmask[k * 16 : k * 16 + 16, t * 128 : t * 128 + 128] = jnp.where(low16, a, b)
    parts = lm_ref[0, 192:208, :].astype(F32)
    offset_ref[...] = parts[12:13] + parts[13:14] + parts[14:15]
    scale = jnp.concatenate(
        [1.0 / (dot(rmask[zl], lmask[...], NT)[0:24] + 1.0) for zl in range(2)], axis=0
    )

    lanes = lax.broadcasted_iota(jnp.int32, (48, 128), 1)
    half = lanes < 64
    even = (lanes // WIDTH) % 2 == 0
    for pair in range(2):
        rhs = jnp.concatenate(
            [
                jnp.concatenate(
                    [
                        ref[4 * k + t, g * S : g * S + S, :]
                        for k in (2 * pair, 2 * pair + 1)
                        for g in range(3)
                    ],
                    axis=1,
                )
                for t in range(4)
                for ref in (lm_ref, lo_ref)
            ],
            axis=0,
        )
        outer = [dot(rt[zl], rhs) for zl in range(2)]
        for n in range(2):
            left_rows = []
            for g in range(3 * n, 3 * n + 3):
                cols = slice(g * 128, g * 128 + 128)
                quads = [[], [], [], []]
                for q in range(4):
                    a = [
                        jnp.concatenate([o[e * 24 : e * 24 + 24, cols] for o in outer], axis=0)
                        .astype(BF16)
                        for e in range(4 * q, 4 * q + 4)
                    ]
                    r02 = pltpu.roll(jnp.where(half, a[2], a[0]), 64, 1)
                    r13 = pltpu.roll(jnp.where(half, a[3], a[1]), 64, 1)
                    a0, a2 = jnp.where(half, a[0], r02), jnp.where(half, r02, a[2])
                    a1, a3 = jnp.where(half, a[1], r13), jnp.where(half, r13, a[3])
                    quads[0].append(jnp.where(even, a0, pltpu.roll(a1, 32, 1)))
                    quads[1].append(jnp.where(even, pltpu.roll(a0, 96, 1), a1))
                    quads[2].append(jnp.where(even, a2, pltpu.roll(a3, 32, 1)))
                    quads[3].append(jnp.where(even, pltpu.roll(a2, 96, 1), a3))
                left_rows += [jnp.concatenate(quad, axis=1) for quad in quads]
            wide = dot(jnp.concatenate(left_rows, axis=0), w_ref[...])
            k = 2 * pair + n
            for i in range(I):
                column = scale[:, k * 16 + i : k * 16 + i + 1]
                for e in range(2):
                    z[e, i * 48 : i * 48 + 48, :] = (
                        wide[i * 48 : i * 48 + 48, e * 128 : e * 128 + 128] * column
                    )
            result = z[0, pl.ds(0, 288, stride=2), :] + z[1, pl.ds(1, 288, stride=2), :]
            out_ref[(x - k) & 3] = result.astype(BF16)


def finish_kernel(pair_ref, offset_ref, out_ref):
    offset = offset_ref[...]
    for x1 in range(4):
        block = pair_ref[x1].astype(F32) + offset
        for i in range(I):
            for zl in range(2):
                at, row = (zl * 4 + x1) * I, (2 * i + zl) * I
                out_ref[i, at : at + I, :] = block[row : row + I, :]


def swap(match):
    index = np.arange(int(np.prod(SIZES))).reshape(SIZES)
    return [(int(index[at]), int(index[match(*at)])) for at in np.ndindex(*SIZES)]


def shifted(y, zl, x, zh, c):
    shift, target = placed((2 * zh + zl - y // 2 * 2) % 8, c)
    return (y + shift) % 8, int(target), x, y // 2, y % 2


TRANSPOSE = swap(shifted)
ALONG_X = [swap(lambda y, zl, x, zh, c, k=k: (y, zl, (x + k) % 4, zh, c)) for k in range(4)]
ACROSS_ZH = [swap(lambda y, zl, x, zh, c, k=k: (y, zl, x, zh ^ k, c)) for k in range(4)]
OTHER_CORE = swap(lambda y, zl, x, zh, c: (y, zl, x, zh, 1 - c))


def spread_along(value, axis, count):
    return lax.all_to_all(
        jnp.broadcast_to(value[None], (count,) + value.shape), axis, 0, 0, tiled=True
    )


def stay(value):
    return pltpu.with_memory_space_constraint(value, pltpu.HBM)


def call(kernel, out_shape, in_specs, scratch_shapes=(), vmem=48, flops=0, bytes_accessed=0):
    return pl.pallas_call(
        kernel,
        out_shape=out_shape,
        in_specs=in_specs,
        out_specs=jax.tree.map(lambda _: VMEM, out_shape),
        scratch_shapes=scratch_shapes,
        compiler_params=pltpu.CompilerParams(vmem_limit_bytes=vmem << 20),
        cost_estimate=pl.CostEstimate(
            flops=flops, bytes_accessed=bytes_accessed, transcendentals=0
        ),
    )


def local(x, m, wl, wr, w, offset):
    left, right = call(
        project_kernel,
        [
            jax.ShapeDtypeStruct((1, ROWS, 128), BF16),
            jax.ShapeDtypeStruct((ROWS, 128), BF16),
        ],
        [HBM] * 5,
        [
            pltpu.VMEM((I, S, C), BF16),
            pltpu.VMEM((I, S), jnp.int32),
            pltpu.VMEM((WIDTH, C), BF16),
            pltpu.VMEM((WIDTH, C), BF16),
            pltpu.VMEM((1, PAIR), F32),
            pltpu.VMEM((192, 128), F32),
            pltpu.SemaphoreType.DMA((5,)),
        ],
    )(*map(stay, (x.transpose(1, 0, 2), m.T, wl.T, wr.T, offset.reshape(1, PAIR))))
    w2 = w.reshape(WIDTH, 16, 2, PAIR).transpose(1, 0, 2, 3).reshape(512, 2 * PAIR)
    at = jnp.stack([lax.axis_index(name) for name in ("zh", "core", "x")]).astype(jnp.int32)

    right = lax.ppermute(right, AXES, TRANSPOSE)
    right = jnp.broadcast_to(right[None], (16, ROWS, 128))
    left = lax.optimization_barrier(
        jnp.concatenate([left, lax.ppermute(left, AXES, ACROSS_ZH[2])])
    )
    left = jnp.concatenate([left, lax.ppermute(left, AXES, ACROSS_ZH[1])])
    left = lax.optimization_barrier((left, right))[0]
    right = lax.all_to_all(right, ("y", "zl"), 0, 0, tiled=True)
    along = {k: lax.ppermute(left, AXES, ALONG_X[k]) for k in (2, 3, 1)}
    left = jnp.concatenate([left, along[1], along[2], along[3]], axis=0)
    left_other = lax.ppermute(left, AXES, OTHER_CORE)

    pairs, offset = call(
        pair_kernel,
        [jax.ShapeDtypeStruct((4, 288, 128), BF16), jax.ShapeDtypeStruct((1, PAIR), F32)],
        [SMEM] + [VMEM] * 4,
        [
            pltpu.VMEM((2, 384, 512), BF16),
            pltpu.VMEM((2, 32, 512), BF16),
            pltpu.VMEM((64, 512), BF16),
            pltpu.VMEM((2, 576, 128), F32),
        ],
        flops=3 << 30,
        bytes_accessed=4 << 20,
    )(at, right, w2, left, left_other)
    pairs = lax.all_to_all(pairs, "x", 0, 0, tiled=True)
    return call(
        finish_kernel, jax.ShapeDtypeStruct((I, 96, PAIR), F32), [VMEM, VMEM]
    )(pairs, offset)


def solution(mesh):
    fine = Mesh(mesh.devices.reshape(SIZES), AXES)
    res, seq = ("y", "zl", "x"), ("zh", "core")
    return jax.shard_map(
        local,
        mesh=fine,
        in_specs=(P(seq, res, None), P(seq, res), P(), P(), P(), P()),
        out_specs=P(res, seq, None),
        check_vma=False,
    )
```

```python
import numpy as np

import jax
import jax.numpy as jnp
from jax import lax
from jax.experimental import pallas as pl
from jax.experimental.pallas import tpu as pltpu
from jax.sharding import Mesh
from jax.sharding import PartitionSpec as P

F32, BF16 = jnp.float32, jnp.bfloat16
SIZES = (8, 2, 4, 4, 2)
AXES = ("y", "zl", "x", "zh", "core")
S, I, C, WIDTH, PAIR = 64, 12, 256, 32, 128
SENT_ROWS = 320
ROWS = 200
NT = (((1,), (1,)), ((), ()))
VMEM = pl.BlockSpec(memory_space=pltpu.VMEM)
HBM = pl.BlockSpec(memory_space=pltpu.HBM)
SMEM = pl.BlockSpec(memory_space=pltpu.SMEM)


def one_hot(shape, match):
    row = lax.broadcasted_iota(jnp.int32, shape, 0)
    col = lax.broadcasted_iota(jnp.int32, shape, 1)
    return match(row, col).astype(F32).astype(BF16)


def dot(a, b, dims=(((1,), (0,)), ((), ()))):
    return lax.dot_general(a, b, dims, preferred_element_type=F32)


def project_kernel(
    x_in, m_in, wl_in, wr_in, offset_in, l_ref, l2_ref, r_ref, x_ref, m_ref, wl_ref, wr_ref, offset_ref, spread, sems
):
    pairs = [
        (x_in, x_ref), (m_in, m_ref), (wl_in, wl_ref), (wr_in, wr_ref), (offset_in, offset_ref)
    ]
    copies = [
        pltpu.make_async_copy(source, target, sems.at[n])
        for n, (source, target) in enumerate(pairs)
    ]
    for copy in copies:
        copy.start()
    for copy in copies:
        copy.wait()
    mask = m_ref[...].astype(F32).astype(BF16)
    mask_twice = jnp.concatenate([mask, mask], axis=1)
    mask_halves = [dot(one_hot((8, I), lambda r, t: (t == r + h) & (r < 6)), mask_twice) for h in (0, 6)]
    mask_cols = dot(one_hot((S, S), lambda r, t: r == t), mask, NT)
    wl = dot(one_hot((128, WIDTH), lambda r, t: r % WIDTH == t), wl_ref[...])
    wr = dot(
        one_hot((128, WIDTH), lambda r, t: t == 2 * (r % 16) + r % WIDTH // 16), wr_ref[...]
    )
    weights = jnp.concatenate([wl, wr], axis=0).astype(BF16)
    block = lax.broadcasted_iota(jnp.int32, (S, 256), 1) % 128 // WIDTH
    low = lax.broadcasted_iota(jnp.int32, (8, 128), 1) < 64
    tiles = []
    for g in range(I // 4):
        x = x_ref[4 * g : 4 * g + 4].reshape(4 * S, C).astype(F32)
        centred = x - jnp.sum(x, axis=-1, keepdims=True) * (1.0 / C)
        variance = jnp.sum(centred * centred, axis=-1, keepdims=True) * (1.0 / C)
        normed = centred * lax.rsqrt(variance + 1e-05)
        high = normed.astype(BF16)
        rest = (normed - high.astype(F32)).astype(BF16)
        both = dot(high, weights, NT) + dot(rest, weights, NT)
        tile = None
        for k in range(4):
            i = 4 * g + k
            part = both[k * S : k * S + S] * mask_cols[:, i : i + 1]
            tile = part if k == 0 else jnp.where(block == k, part, tile)
        tiles.append(tile[:, 0:128])
        right = tile[:, 128:256]
        right = jnp.concatenate([right, right], axis=0).T
        for k in range(4):
            for e in range(2):
                row = k * WIDTH + e * 16
                part = jnp.where(low, right[row : row + 8], right[row + 8 : row + 16])
                spread[pl.ds(2 * (4 * g + k) + e, 8, stride=24), :] = part
    mask_block = jnp.where(low, mask_halves[0], mask_halves[1])
    row = lax.broadcasted_iota(jnp.int32, (8, 128), 0)
    rest, parts = offset_ref[...], []
    for n in range(3):
        part = rest.astype(BF16).astype(F32)
        parts.append(jnp.broadcast_to(part, (8, 128)))
        rest = rest - part
    last = jnp.where(row == 6, parts[0], jnp.where(row == 7, parts[1], mask_block))
    left = jnp.concatenate([jnp.concatenate(tiles, axis=0), last], axis=0).astype(BF16)
    l_ref[0] = left
    r_ref[192:SENT_ROWS, :] = jnp.zeros((SENT_ROWS - 192, 128), BF16)
    l2_ref[0] = left
    l2_ref[1] = jnp.zeros((ROWS, 128), BF16)
    last = jnp.where(row == 6, parts[2], mask_block)
    r_ref[0:ROWS, :] = jnp.concatenate([spread[...], last], axis=0).astype(BF16)


def placed(step, core):
    zl = (step >= 1) & (step <= 4)
    far = zl * (step - 1) + (1 - zl) * ((8 - step) & 7)
    return core * (3 - far) + (1 - core) * (4 + far), zl


def pair_kernel(at_ref, r_ref, w_ref, lm_ref, lo_ref, out_ref, offset_ref, rt, rmask, lmask, z):
    zh, core, x = at_ref[0], at_ref[1], at_ref[2]
    low = lax.broadcasted_iota(jnp.int32, (ROWS, 128), 1) < 64
    low8 = lax.broadcasted_iota(jnp.int32, (8, 128), 1) < 64

    def piece(zl, t, c):
        step = (2 * ((zh ^ (0, 2, 1, 3)[t]) - zh) + zl) & 7
        target = jnp.where((step >= 1) & (step <= 4), 1, 0)
        far = jnp.where(target == 1, step - 1, (8 - step) & 7)
        shift = jnp.where(c == 1, 3 - far, 4 + far)
        return r_ref[((2 * zh + core + shift) & 7) * 2 + target]

    for zl in range(2):
        for t in range(4):
            a, b = piece(zl, t, core), piece(zl, t, 1 - core)
            first = jnp.where(low, a, pltpu.roll(b, 64, 1))
            second = jnp.where(low, pltpu.roll(a, 64, 1), b)
            cols = slice(t * 128, t * 128 + 128)
            rt[zl, 0:192, cols] = first[0:192]
            rt[zl, 192:384, cols] = second[0:192]
            rmask[zl, :, cols] = jnp.concatenate([first[192:200], second[192:200]], axis=0)
    for k in range(4):
        for t in range(4):
            a, b = lm_ref[4 * k + t][192:200], lo_ref[4 * k + t][192:200]
            lmask[k * 16 : k * 16 + 16, t * 128 : t * 128 + 128] = jnp.concatenate(
                [
                    jnp.where(low8, a, pltpu.roll(b, 64, 1)),
                    jnp.where(low8, pltpu.roll(a, 64, 1), b),
                ],
                axis=0,
            )
    parts = lm_ref[0][192:200].astype(F32)
    offset_ref[...] = parts[6:7] + parts[7:8] + r_ref[0][192:200].astype(F32)[6:7]
    twice = one_hot((24, 16), lambda r, t: t == r // 2 + jnp.where(r < 12, 0, 2))
    scale = jnp.concatenate(
        [
            1.0 / (dot(dot(twice, rmask[zl]).astype(BF16), lmask[...], NT) + 1.0)
            for zl in range(2)
        ],
        axis=0,
    )

    lanes = lax.broadcasted_iota(jnp.int32, (48, 128), 1)
    half = lanes < 64
    even = (lanes // WIDTH) % 2 == 0
    for pair in range(2):
        rhs = jnp.concatenate(
            [
                jnp.concatenate(
                    [
                        ref[4 * k + t, g * S : g * S + S, :]
                        for k in (2 * pair, 2 * pair + 1)
                        for g in range(3)
                    ],
                    axis=1,
                )
                for t in range(4)
                for ref in (lm_ref, lo_ref)
            ],
            axis=0,
        )
        outer = [dot(rt[zl], rhs) for zl in range(2)]
        for n in range(2):
            left_rows = []
            for g in range(3 * n, 3 * n + 3):
                cols = slice(g * 128, g * 128 + 128)
                quads = [[], [], [], []]
                for q in range(4):
                    a = [
                        jnp.concatenate([o[e * 24 : e * 24 + 24, cols] for o in outer], axis=0)
                        .astype(BF16)
                        for e in range(4 * q, 4 * q + 4)
                    ]
                    r02 = pltpu.roll(jnp.where(half, a[2], a[0]), 64, 1)
                    r13 = pltpu.roll(jnp.where(half, a[3], a[1]), 64, 1)
                    a0, a2 = jnp.where(half, a[0], r02), jnp.where(half, r02, a[2])
                    a1, a3 = jnp.where(half, a[1], r13), jnp.where(half, r13, a[3])
                    quads[0].append(jnp.where(even, a0, pltpu.roll(a1, 32, 1)))
                    quads[1].append(jnp.where(even, pltpu.roll(a0, 96, 1), a1))
                    quads[2].append(jnp.where(even, a2, pltpu.roll(a3, 32, 1)))
                    quads[3].append(jnp.where(even, pltpu.roll(a2, 96, 1), a3))
                left_rows += [jnp.concatenate(quad, axis=1) for quad in quads]
            wide = dot(jnp.concatenate(left_rows, axis=0), w_ref[...])
            k = 2 * pair + n
            for i in range(I):
                at = k * 16 + i + (0 if i < 6 else 2)
                column = scale[:, at : at + 1]
                for e in range(2):
                    z[e, i * 48 : i * 48 + 48, :] = (
                        wide[i * 48 : i * 48 + 48, e * 128 : e * 128 + 128] * column
                    )
            result = z[0, pl.ds(0, 288, stride=2), :] + z[1, pl.ds(1, 288, stride=2), :]
            out_ref[(x - k) & 3] = result.astype(BF16)


def finish_kernel(pair_ref, offset_ref, out_ref):
    offset = offset_ref[...]
    for x1 in range(4):
        block = pair_ref[x1].astype(F32) + offset
        for i in range(I):
            for zl in range(2):
                at, row = (zl * 4 + x1) * I, (2 * i + zl) * I
                out_ref[i, at : at + I, :] = block[row : row + I, :]


def swap(match):
    index = np.arange(int(np.prod(SIZES))).reshape(SIZES)
    return [(int(index[at]), int(index[match(*at)])) for at in np.ndindex(*SIZES)]


def shifted(y, zl, x, zh, c):
    shift, target = placed((2 * zh + zl - y // 2 * 2) % 8, c)
    return (y + shift) % 8, int(target), x, y // 2, y % 2


TRANSPOSE = swap(shifted)
ALONG_X = [swap(lambda y, zl, x, zh, c, k=k: (y, zl, (x + k) % 4, zh, c)) for k in range(4)]
ACROSS_ZH = [swap(lambda y, zl, x, zh, c, k=k: (y, zl, x, zh ^ k, c)) for k in range(4)]
OTHER_CORE = swap(lambda y, zl, x, zh, c: (y, zl, x, zh, 1 - c))


def spread_along(value, axis, count):
    return lax.all_to_all(
        jnp.broadcast_to(value[None], (count,) + value.shape), axis, 0, 0, tiled=True
    )


def stay(value):
    return pltpu.with_memory_space_constraint(value, pltpu.HBM)


def call(kernel, out_shape, in_specs, scratch_shapes=(), vmem=48, flops=0, bytes_accessed=0):
    return pl.pallas_call(
        kernel,
        out_shape=out_shape,
        in_specs=in_specs,
        out_specs=jax.tree.map(lambda _: VMEM, out_shape),
        scratch_shapes=scratch_shapes,
        compiler_params=pltpu.CompilerParams(vmem_limit_bytes=vmem << 20),
        cost_estimate=pl.CostEstimate(
            flops=flops, bytes_accessed=bytes_accessed, transcendentals=0
        ),
    )


def local(x, m, wl, wr, w, offset):
    left, lefts, right = call(
        project_kernel,
        [
            jax.ShapeDtypeStruct((1, ROWS, 128), BF16),
            jax.ShapeDtypeStruct((2, ROWS, 128), BF16),
            jax.ShapeDtypeStruct((SENT_ROWS, 128), BF16),
        ],
        [HBM] * 5,
        [
            pltpu.VMEM((I, S, C), BF16),
            pltpu.VMEM((I, S), jnp.int32),
            pltpu.VMEM((WIDTH, C), BF16),
            pltpu.VMEM((WIDTH, C), BF16),
            pltpu.VMEM((1, PAIR), F32),
            pltpu.VMEM((192, 128), F32),
            pltpu.SemaphoreType.DMA((5,)),
        ],
    )(*map(stay, (x.transpose(1, 0, 2), m.T, wl.T, wr.T, offset.reshape(1, PAIR))))
    w2 = w.reshape(WIDTH, 16, 2, PAIR).transpose(1, 0, 2, 3).reshape(512, 2 * PAIR)
    at = jnp.stack([lax.axis_index(name) for name in ("zh", "core", "x")]).astype(jnp.int32)

    right = lax.ppermute(right, AXES, TRANSPOSE)
    right = jnp.broadcast_to(right[None, :ROWS], (16, ROWS, 128))
    far = lax.ppermute(left, AXES, ACROSS_ZH[2])
    left = lax.dynamic_update_slice(lefts, far, (1, 0, 0))
    left = jnp.concatenate([left, lax.ppermute(left, AXES, ACROSS_ZH[1])])
    left = lax.optimization_barrier((left, right))[0]
    right = lax.all_to_all(right, ("y", "zl"), 0, 0, tiled=True)
    left = jnp.concatenate(
        [left] + [lax.ppermute(left, AXES, ALONG_X[k]) for k in (1, 2, 3)], axis=0
    )
    left_other = lax.ppermute(left, AXES, OTHER_CORE)

    pairs, offset = call(
        pair_kernel,
        [jax.ShapeDtypeStruct((4, 288, 128), BF16), jax.ShapeDtypeStruct((1, PAIR), F32)],
        [SMEM] + [VMEM] * 4,
        [
            pltpu.VMEM((2, 384, 512), BF16),
            pltpu.VMEM((2, 16, 512), BF16),
            pltpu.VMEM((64, 512), BF16),
            pltpu.VMEM((2, 576, 128), F32),
        ],
        flops=3 << 30,
        bytes_accessed=4 << 20,
    )(at, right, w2, left, left_other)
    pairs = lax.all_to_all(pairs, "x", 0, 0, tiled=True)
    return call(
        finish_kernel, jax.ShapeDtypeStruct((I, 96, PAIR), F32), [VMEM, VMEM]
    )(pairs, offset)


def solution(mesh):
    fine = Mesh(mesh.devices.reshape(SIZES), AXES)
    res, seq = ("y", "zl", "x"), ("zh", "core")
    return jax.shard_map(
        local,
        mesh=fine,
        in_specs=(P(seq, res, None), P(seq, res), P(), P(), P(), P()),
        out_specs=P(res, seq, None),
        check_vma=False,
    )
```

```python
import numpy as np

import jax
import jax.numpy as jnp
from jax import lax
from jax.experimental import pallas as pl
from jax.experimental.pallas import tpu as pltpu
from jax.sharding import Mesh
from jax.sharding import PartitionSpec as P

F32, BF16 = jnp.float32, jnp.bfloat16
SIZES = (8, 2, 4, 4, 2)
AXES = ("y", "zl", "x", "zh", "core")
S, I, C, WIDTH, PAIR = 64, 12, 256, 32, 128
ROWS = 208
NT = (((1,), (1,)), ((), ()))
VMEM = pl.BlockSpec(memory_space=pltpu.VMEM)
HBM = pl.BlockSpec(memory_space=pltpu.HBM)
SMEM = pl.BlockSpec(memory_space=pltpu.SMEM)


def one_hot(shape, match):
    row = lax.broadcasted_iota(jnp.int32, shape, 0)
    col = lax.broadcasted_iota(jnp.int32, shape, 1)
    return match(row, col).astype(F32).astype(BF16)


def dot(a, b, dims=(((1,), (0,)), ((), ()))):
    return lax.dot_general(a, b, dims, preferred_element_type=F32)


def project_kernel(
    x_in, m_in, wl_in, wr_in, offset_in, l_ref, r_ref, x_ref, m_ref, wl_ref, wr_ref, offset_ref, spread, sems
):
    pairs = [
        (x_in, x_ref), (m_in, m_ref), (wl_in, wl_ref), (wr_in, wr_ref), (offset_in, offset_ref)
    ]
    copies = [
        pltpu.make_async_copy(source, target, sems.at[n])
        for n, (source, target) in enumerate(pairs)
    ]
    for copy in copies:
        copy.start()
    for copy in copies:
        copy.wait()
    mask = m_ref[...].astype(F32).astype(BF16)
    mask_twice = jnp.concatenate([mask, mask], axis=1)
    mask_rows = dot(one_hot((16, I), lambda r, t: r == t), mask_twice)
    mask_pairs = dot(one_hot((32, I), lambda r, t: r // 2 == t), mask_twice)
    mask_cols = dot(one_hot((S, S), lambda r, t: r == t), mask, NT)
    wl = dot(one_hot((128, WIDTH), lambda r, t: r % WIDTH == t), wl_ref[...])
    wr = dot(
        one_hot((128, WIDTH), lambda r, t: t == 2 * (r % 16) + r % WIDTH // 16), wr_ref[...]
    )
    weights = jnp.concatenate([wl, wr], axis=0).astype(BF16)
    block = lax.broadcasted_iota(jnp.int32, (S, 256), 1) % 128 // WIDTH
    low = lax.broadcasted_iota(jnp.int32, (8, 128), 1) < 64
    for g in range(I // 4):
        x = x_ref[4 * g : 4 * g + 4].reshape(4 * S, C).astype(F32)
        centred = x - jnp.sum(x, axis=-1, keepdims=True) * (1.0 / C)
        variance = jnp.sum(centred * centred, axis=-1, keepdims=True) * (1.0 / C)
        normed = centred * lax.rsqrt(variance + 1e-05)
        high = normed.astype(BF16)
        rest = (normed - high.astype(F32)).astype(BF16)
        both = dot(high, weights, NT) + dot(rest, weights, NT)
        tile = None
        for k in range(4):
            i = 4 * g + k
            part = both[k * S : k * S + S] * mask_cols[:, i : i + 1]
            tile = part if k == 0 else jnp.where(block == k, part, tile)
        l_ref[0, g * S : (g + 1) * S, :] = tile[:, 0:128].astype(BF16)
        right = tile[:, 128:256]
        right = jnp.concatenate([right, right], axis=0).T
        for k in range(4):
            for e in range(2):
                row = k * WIDTH + e * 16
                part = jnp.where(low, right[row : row + 8], right[row + 8 : row + 16])
                spread[pl.ds(2 * (4 * g + k) + e, 8, stride=24), :] = part
    row = lax.broadcasted_iota(jnp.int32, (16, 128), 0)
    last, rest = mask_rows, offset_ref[...]
    for n in range(3):
        part = rest.astype(BF16).astype(F32)
        last = jnp.where(row == I + n, jnp.broadcast_to(part, (16, 128)), last)
        rest = rest - part
    l_ref[0, 192:208, :] = last.astype(BF16)
    r_ref[0:192, :] = spread[...].astype(BF16)
    low16 = lax.broadcasted_iota(jnp.int32, (16, 128), 1) < 64
    r_ref[192:208, :] = jnp.where(low16, mask_pairs[0:16], mask_pairs[16:32]).astype(BF16)


def placed(step, core):
    zl = (step >= 1) & (step <= 4)
    far = zl * (step - 1) + (1 - zl) * ((8 - step) & 7)
    return core * (3 - far) + (1 - core) * (4 + far), zl


def pair_kernel(at_ref, r_ref, w_ref, lm_ref, lo_ref, out_ref, offset_ref, rt, rmask, lmask, z):
    zh, core, x = at_ref[0], at_ref[1], at_ref[2]
    low = lax.broadcasted_iota(jnp.int32, (ROWS, 128), 1) < 64
    low16 = lax.broadcasted_iota(jnp.int32, (16, 128), 1) < 64

    def piece(zl, t, c):
        step = (2 * ((zh ^ (0, 2, 1, 3)[t]) - zh) + zl) & 7
        target = jnp.where((step >= 1) & (step <= 4), 1, 0)
        far = jnp.where(target == 1, step - 1, (8 - step) & 7)
        shift = jnp.where(c == 1, 3 - far, 4 + far)
        return r_ref[((2 * zh + core + shift) & 7) * 2 + target]

    for zl in range(2):
        for t in range(4):
            a, b = piece(zl, t, core), piece(zl, t, 1 - core)
            first = jnp.where(low, a, pltpu.roll(b, 64, 1))
            second = jnp.where(low, pltpu.roll(a, 64, 1), b)
            cols = slice(t * 128, t * 128 + 128)
            rt[zl, 0:192, cols] = first[0:192]
            rt[zl, 192:384, cols] = second[0:192]
            rmask[zl, 0:16, cols] = first[192:208]
            rmask[zl, 16:32, cols] = second[192:208]
    for k in range(4):
        for t in range(4):
            a, b = lm_ref[4 * k + t, 192:208, :], lo_ref[4 * k + t, 192:208, :]
            lmask[k * 16 : k * 16 + 16, t * 128 : t * 128 + 128] = jnp.where(low16, a, b)
    parts = lm_ref[0, 192:208, :].astype(F32)
    offset_ref[...] = parts[12:13] + parts[13:14] + parts[14:15]
    scale = jnp.concatenate(
        [1.0 / (dot(rmask[zl], lmask[...], NT)[0:24] + 1.0) for zl in range(2)], axis=0
    )

    lanes = lax.broadcasted_iota(jnp.int32, (48, 128), 1)
    half = lanes < 64
    even = (lanes // WIDTH) % 2 == 0
    for pair in range(2):
        rhs = jnp.concatenate(
            [
                jnp.concatenate(
                    [
                        ref[4 * k + t, g * S : g * S + S, :]
                        for k in (2 * pair, 2 * pair + 1)
                        for g in range(3)
                    ],
                    axis=1,
                )
                for t in range(4)
                for ref in (lm_ref, lo_ref)
            ],
            axis=0,
        )
        outer = [dot(rt[zl], rhs).astype(BF16) for zl in range(2)]
        for n in range(2):
            left_rows = []
            for g in range(3 * n, 3 * n + 3):
                cols = slice(g * 128, g * 128 + 128)
                quads = [[], [], [], []]
                for q in range(4):
                    a = [
                        jnp.concatenate([o[e * 24 : e * 24 + 24, cols] for o in outer], axis=0)
                        for e in range(4 * q, 4 * q + 4)
                    ]
                    r02 = pltpu.roll(jnp.where(half, a[2], a[0]), 64, 1)
                    r13 = pltpu.roll(jnp.where(half, a[3], a[1]), 64, 1)
                    a0, a2 = jnp.where(half, a[0], r02), jnp.where(half, r02, a[2])
                    a1, a3 = jnp.where(half, a[1], r13), jnp.where(half, r13, a[3])
                    quads[0].append(jnp.where(even, a0, pltpu.roll(a1, 32, 1)))
                    quads[1].append(jnp.where(even, pltpu.roll(a0, 96, 1), a1))
                    quads[2].append(jnp.where(even, a2, pltpu.roll(a3, 32, 1)))
                    quads[3].append(jnp.where(even, pltpu.roll(a2, 96, 1), a3))
                left_rows += [jnp.concatenate(quad, axis=1) for quad in quads]
            wide = dot(jnp.concatenate(left_rows, axis=0), w_ref[...])
            k = 2 * pair + n
            for i in range(I):
                column = scale[:, k * 16 + i : k * 16 + i + 1]
                for e in range(2):
                    z[e, i * 48 : i * 48 + 48, :] = (
                        wide[i * 48 : i * 48 + 48, e * 128 : e * 128 + 128] * column
                    )
            result = z[0, pl.ds(0, 288, stride=2), :] + z[1, pl.ds(1, 288, stride=2), :]
            out_ref[(x - k) & 3] = result.astype(BF16)


def finish_kernel(pair_ref, offset_ref, out_ref):
    offset = offset_ref[...]
    for x1 in range(4):
        block = pair_ref[x1].astype(F32) + offset
        for i in range(I):
            for zl in range(2):
                at, row = (zl * 4 + x1) * I, (2 * i + zl) * I
                out_ref[i, at : at + I, :] = block[row : row + I, :]


def swap(match):
    index = np.arange(int(np.prod(SIZES))).reshape(SIZES)
    return [(int(index[at]), int(index[match(*at)])) for at in np.ndindex(*SIZES)]


def shifted(y, zl, x, zh, c):
    shift, target = placed((2 * zh + zl - y // 2 * 2) % 8, c)
    return (y + shift) % 8, int(target), x, y // 2, y % 2


TRANSPOSE = swap(shifted)
ALONG_X = [swap(lambda y, zl, x, zh, c, k=k: (y, zl, (x + k) % 4, zh, c)) for k in range(4)]
ACROSS_ZH = [swap(lambda y, zl, x, zh, c, k=k: (y, zl, x, zh ^ k, c)) for k in range(4)]
OTHER_CORE = swap(lambda y, zl, x, zh, c: (y, zl, x, zh, 1 - c))


def spread_along(value, axis, count):
    return lax.all_to_all(
        jnp.broadcast_to(value[None], (count,) + value.shape), axis, 0, 0, tiled=True
    )


def stay(value):
    return pltpu.with_memory_space_constraint(value, pltpu.HBM)


def call(kernel, out_shape, in_specs, scratch_shapes=(), vmem=48, flops=0, bytes_accessed=0):
    return pl.pallas_call(
        kernel,
        out_shape=out_shape,
        in_specs=in_specs,
        out_specs=jax.tree.map(lambda _: VMEM, out_shape),
        scratch_shapes=scratch_shapes,
        compiler_params=pltpu.CompilerParams(vmem_limit_bytes=vmem << 20),
        cost_estimate=pl.CostEstimate(
            flops=flops, bytes_accessed=bytes_accessed, transcendentals=0
        ),
    )


def local(x, m, wl, wr, w, offset):
    left, right = call(
        project_kernel,
        [
            jax.ShapeDtypeStruct((1, ROWS, 128), BF16),
            jax.ShapeDtypeStruct((ROWS, 128), BF16),
        ],
        [HBM] * 5,
        [
            pltpu.VMEM((I, S, C), BF16),
            pltpu.VMEM((I, S), jnp.int32),
            pltpu.VMEM((WIDTH, C), BF16),
            pltpu.VMEM((WIDTH, C), BF16),
            pltpu.VMEM((1, PAIR), F32),
            pltpu.VMEM((192, 128), F32),
            pltpu.SemaphoreType.DMA((5,)),
        ],
    )(*map(stay, (x.transpose(1, 0, 2), m.T, wl.T, wr.T, offset.reshape(1, PAIR))))
    w2 = w.reshape(WIDTH, 16, 2, PAIR).transpose(1, 0, 2, 3).reshape(512, 2 * PAIR)
    at = jnp.stack([lax.axis_index(name) for name in ("zh", "core", "x")]).astype(jnp.int32)

    right = lax.ppermute(right, AXES, TRANSPOSE)
    right = jnp.broadcast_to(right[None], (16, ROWS, 128))
    left = lax.optimization_barrier(
        jnp.concatenate([left, lax.ppermute(left, AXES, ACROSS_ZH[2])])
    )
    left = jnp.concatenate([left, lax.ppermute(left, AXES, ACROSS_ZH[1])])
    left = lax.optimization_barrier((left, right))[0]
    right = lax.all_to_all(right, ("y", "zl"), 0, 0, tiled=True)
    along = {k: lax.ppermute(left, AXES, ALONG_X[k]) for k in (2, 3, 1)}
    left = jnp.concatenate([left, along[1], along[2], along[3]], axis=0)
    left_other = lax.ppermute(left, AXES, OTHER_CORE)

    pairs, offset = call(
        pair_kernel,
        [jax.ShapeDtypeStruct((4, 288, 128), BF16), jax.ShapeDtypeStruct((1, PAIR), F32)],
        [SMEM] + [VMEM] * 4,
        [
            pltpu.VMEM((2, 384, 512), BF16),
            pltpu.VMEM((2, 32, 512), BF16),
            pltpu.VMEM((64, 512), BF16),
            pltpu.VMEM((2, 576, 128), F32),
        ],
        flops=3 << 30,
        bytes_accessed=4 << 20,
    )(at, right, w2, left, left_other)
    pairs = lax.all_to_all(pairs, "x", 0, 0, tiled=True)
    return call(
        finish_kernel, jax.ShapeDtypeStruct((I, 96, PAIR), F32), [VMEM, VMEM]
    )(pairs, offset)


def solution(mesh):
    fine = Mesh(mesh.devices.reshape(SIZES), AXES)
    res, seq = ("y", "zl", "x"), ("zh", "core")
    return jax.shard_map(
        local,
        mesh=fine,
        in_specs=(P(seq, res, None), P(seq, res), P(), P(), P(), P()),
        out_specs=P(res, seq, None),
        check_vma=False,
    )
```
